128 devices in a mesh: row: 8 (over x, core), col: 16 (over y, z).
Axes of the slice: x: 4, y: 4, z: 4, core: 2. Of those that a mesh axis runs over, the one named last changes fastest.
Arguments:
- features: bfloat16 [65536, 256], P(('row', 'col')), may hold values from -6 to 6
- weight: bfloat16 [256, 256], replicated, may hold values from -0.375 to 0.375
- cotangent: bfloat16 [65536, 256], P(('row', 'col')), may hold values from -6 to 6
- tile_values: bfloat16 [8, 16, 384, 128, 128], P('row', 'col'), may hold values from 0 to 0.15, as said below
- tile_rows: int32 [8, 16, 384], P('row', 'col'), may hold values from 0 to 63
- tile_cols: int32 [8, 16, 384], P('row', 'col'), may hold values from 0 to 31
- tile_count: int32 [8, 16], P('row', 'col'), may hold values from 96 to 384, as said below
Outputs:
- activated: bfloat16 [65536, 256], P(('row', 'col'))
- grad_features: bfloat16 [65536, 256], P(('row', 'col'))
- grad_weight: float32 [256, 256], replicated
The draws below stay inside these ranges and needn't reach their ends.
Inputs may be any that keep to these rules, and one draw needn't show every extreme that they name: `tile_count`: some device in every draw has all 384 slots live. `tile_values`: each entry is zero or a positive edge weight.
All inputs are finite; a program needn't handle non-finite values.
Results may differ from the reference program's by a relative error of at most 0.006.
Values may be sent and summed in bfloat16 or wider, within the bound.
No kernel may reach another device: no remote copies, remote signals or barrier semaphores. Data moves between devices by JAX's collectives and lax.ppermute only.
A program may use at most 128 MiB of HBM per device.

```python
import jax
import jax.numpy as jnp
from jax import lax

F = 256
BLOCK = 128
BPS = 4
TILES_DEV = 384
NODES = 65536
ROW_BLOCKS = 64
COL_BLOCKS = 32
N_ROW = 8
N_COL = 16


def draw_tile_count(key, part):
    key = jax.random.fold_in(key, 7)
    first, second = jax.random.split(key)
    counts = jax.random.randint(first, (N_ROW, N_COL), TILES_DEV // 4, TILES_DEV + 1)
    chosen = jax.random.randint(second, (), 0, N_ROW * N_COL)
    flat_ids = jnp.arange(N_ROW * N_COL).reshape(N_ROW, N_COL)
    return jnp.where(flat_ids == chosen, TILES_DEV, counts).astype(jnp.int32)


def draw_tile_values(key, part):
    key = jax.random.fold_in(key, 11)
    first, second = jax.random.split(key)
    shape = (N_ROW, N_COL, TILES_DEV, BLOCK, BLOCK)
    present = jax.random.uniform(first, shape, jnp.float32) < 1.0 / (4.0 * BLOCK)
    magnitude = jnp.exp(jax.random.uniform(second, shape, jnp.float32, jnp.log(0.03), jnp.log(0.1494)))
    return jnp.where(present, magnitude, 0.0).astype(jnp.bfloat16)


def plant(drawn, key, low, largest):
    dims = drawn.shape
    index_at = [jax.random.randint(jax.random.fold_in(key, axis), (), 0, dims[axis]) for axis in range(len(dims))]
    drawn = drawn.at[tuple(index_at)].set(low)
    longest = dims.index(max(dims))
    index_at[longest] = (index_at[longest] + 1) % dims[longest]
    return drawn.at[tuple(index_at)].set(largest)


def level_of(key, extent, cuts, smallest, largest):
    def one(dim, parts):
        steps = jax.random.uniform(jax.random.fold_in(jax.random.fold_in(key, 6), dim), (parts,), jnp.float32, smallest / len(cuts), largest / len(cuts))
        return jnp.repeat(jnp.exp(steps), extent[dim] // parts).reshape((-1,) + (1,) * (len(extent) - dim - 1))

    factor_of = one(*cuts[0])
    for cut in cuts[1:]:
        factor_of = factor_of * one(*cut)
    return factor_of


def normal_values(rng, dims, deviation, bound, shards=(), kind=jnp.bfloat16):
    factor_of = level_of(rng, dims, shards, -0.22, 0.18) if shards else 1.0
    drawn = jax.random.normal(rng, dims, jnp.float32) * deviation * factor_of
    return jnp.minimum(jnp.maximum(drawn, -bound), bound).astype(kind)


def setup_inputs(seed: int = 0) -> dict:
    splits = jax.random.split(jax.random.key(seed), 8)
    return {
        "features": normal_values(splits[0], (NODES, F), 1.0, 6.0, ((0, 128),)),
        "weight": normal_values(splits[1], (F, F), F ** -0.5, 0.375),
        "cotangent": normal_values(splits[2], (NODES, F), 1.0, 6.0, ((0, 128),)),
        "tile_values": draw_tile_values(jax.random.fold_in(splits[7], 71), 0),
        "tile_rows": plant(jax.random.randint(splits[4], (N_ROW, N_COL, TILES_DEV), 0, ROW_BLOCKS), jax.random.fold_in(splits[4], 1), 0, ROW_BLOCKS - 1).astype(jnp.int32),
        "tile_cols": plant(jax.random.randint(splits[5], (N_ROW, N_COL, TILES_DEV), 0, COL_BLOCKS), jax.random.fold_in(splits[5], 1), 0, COL_BLOCKS - 1).astype(jnp.int32),
        "tile_count": draw_tile_count(jax.random.fold_in(splits[7], 71), 0),
    }


def gelu_tanh(value):
    return jax.nn.gelu(value, approximate=True)

def aggregate_ref(tile_vals, out_ids, in_ids, source, live_count, out_blocks, flipped):
    tile_size = tile_vals.shape[-1]
    feat_width = source.shape[1]
    picked = source.reshape(-1, tile_size, feat_width)[in_ids].astype(jnp.float32)
    pattern = 'gba,gbf->gaf' if flipped else 'gab,gbf->gaf'
    products = jnp.einsum(pattern, tile_vals.astype(jnp.float32), picked, precision=lax.Precision.HIGHEST)
    live_mask = (jnp.arange(tile_vals.shape[0]) < live_count).astype(jnp.float32)
    products = products * live_mask[:, None, None]
    summed = jax.ops.segment_sum(products, out_ids, num_segments=out_blocks)
    return summed.reshape(out_blocks * tile_size, feat_width)

def reference(features, weight, cotangent, tile_values, tile_rows, tile_cols, tile_count):
    feat_width = features.shape[1]
    slab_rows = BPS * BLOCK
    feat_grid = features.reshape(N_ROW, N_COL, slab_rows, feat_width)

    def forward_one(running, device):
        row_idx = device // N_COL
        col_idx = device % N_COL
        source = lax.dynamic_index_in_dim(feat_grid, col_idx, 1, keepdims=False).reshape(-1, feat_width)
        part = aggregate_ref(tile_values[row_idx, col_idx], tile_rows[row_idx, col_idx], tile_cols[row_idx, col_idx], source, tile_count[row_idx, col_idx], ROW_BLOCKS, False)
        return (running.at[row_idx].add(part), None)
    devices = jnp.arange(N_ROW * N_COL, dtype=jnp.int32)
    start = jnp.zeros((N_ROW, ROW_BLOCKS * BLOCK, feat_width), jnp.float32)
    forward_sum, unused = lax.scan(forward_one, start, devices)
    aggregated = forward_sum.reshape(NODES, feat_width).astype(jnp.bfloat16)
    pre_act = jnp.dot(aggregated, weight, preferred_element_type=jnp.float32)
    activated, pullback = jax.vjp(gelu_tanh, pre_act)
    grad_pre = pullback(cotangent.astype(jnp.float32))[0].astype(jnp.bfloat16)
    mixed = lax.dot_general(grad_pre, weight, (((1,), (1,)), ((), ())), preferred_element_type=jnp.float32).astype(jnp.bfloat16)
    mixed_slabs = mixed.reshape(N_ROW, ROW_BLOCKS * BLOCK, feat_width)

    def backward_one(running, device):
        row_idx = device // N_COL
        col_idx = device % N_COL
        source = lax.dynamic_index_in_dim(mixed_slabs, row_idx, 0, keepdims=False)
        part = aggregate_ref(tile_values[row_idx, col_idx], tile_cols[row_idx, col_idx], tile_rows[row_idx, col_idx], source, tile_count[row_idx, col_idx], COL_BLOCKS, True)
        return (running.at[col_idx].add(part), None)
    start_back = jnp.zeros((N_COL, COL_BLOCKS * BLOCK, feat_width), jnp.float32)
    backward_sum, unused_back = lax.scan(backward_one, start_back, devices)
    arranged = jnp.transpose(backward_sum.reshape(N_COL, N_ROW, slab_rows, feat_width), (1, 0, 2, 3))
    grad_features = arranged.reshape(NODES, feat_width).astype(jnp.bfloat16)
    grad_weight = lax.dot_general(aggregated, grad_pre, (((0,), (0,)), ((), ())), preferred_element_type=jnp.float32)
    return (activated.astype(jnp.bfloat16), grad_features, grad_weight)
```

```python
import math

import jax
import jax.numpy as jnp
from jax import lax
from jax.experimental import pallas as pl
from jax.experimental.pallas import tpu as pltpu
from jax.sharding import PartitionSpec as P

BF = jnp.bfloat16
F32 = jnp.float32
BLK = 128
UNIT = 2
UNROLL = 8
GROUP = UNIT * UNROLL
KEYS = 64
DUMMY = 32

ONE = ((0, 1), (1, 0), (2, 3), (3, 2))
TWO = ((1, 2), (2, 1), (3, 0), (0, 3))
FAR = ((0, 2), (2, 0), (1, 3), (3, 1))


def swap(value, axis, pairs):
    if axis == "z":
        return lax.ppermute(value, "col", [(y * 4 + a, y * 4 + b) for y in range(4) for a, b in pairs])
    if axis == "y":
        return lax.ppermute(value, "col", [(a * 4 + z, b * 4 + z) for z in range(4) for a, b in pairs])
    return lax.ppermute(value, "row", [(a * 2 + k, b * 2 + k) for k in range(2) for a, b in pairs])


def swap_core(value):
    return lax.ppermute(value, "row", [(2 * x + k, 2 * x + 1 - k) for x in range(4) for k in range(2)])


def distance(here, there):
    return jnp.where(here % 2 == 0, there - here, here - there) & 3


def pick(index, table):
    found = jnp.zeros_like(index)
    for place, entry in enumerate(table):
        found = jnp.where(index == place, entry, found)
    return found


ROLE = (6, 1, 0, 4, 7, 5, 2, 3)


def plan(keys, source, live, segments):
    total = keys.shape[0]
    room = -(-(total + KEYS * (UNIT - 1) + len(segments) * GROUP) // GROUP) * GROUP
    keys = jnp.where(live, keys, KEYS)
    all_keys = jnp.arange(KEYS, dtype=jnp.int32)
    segment_of = sum((all_keys >= first).astype(jnp.int32) for first, _ in segments) - 1
    count = jnp.sum((keys[:, None] == all_keys[None, :]).astype(jnp.int32), 0)
    padded = (count + UNIT - 1) // UNIT * UNIT
    before = (all_keys[:, None] < all_keys[None, :]) & (segment_of[:, None] == segment_of[None, :])
    offset = jnp.sum(jnp.where(before, padded[:, None], 0), 0)
    bounds = [jnp.zeros((), jnp.int32)]
    for index, (first, last) in enumerate(segments):
        size = jnp.sum(jnp.where(segment_of == index, padded, 0))
        offset = offset + jnp.where(segment_of == index, bounds[-1] * GROUP, 0)
        bounds.append(bounds[-1] + (size + GROUP - 1) // GROUP)
    slots = jnp.arange(total, dtype=jnp.int32)
    rank = jnp.sum(((keys[:, None] == keys[None, :]) & (slots[None, :] < slots[:, None])).astype(jnp.int32), 1)
    place = rank + jnp.sum(jnp.where(keys[:, None] == all_keys[None, :], offset[None, :], 0), 1)
    place = jnp.where(live, place, -1)
    local = keys
    for first, _ in segments[1:]:
        local = jnp.where(keys >= first, keys - first, local)
    spots = jnp.arange(room, dtype=jnp.int32)
    hit = place[None, :] == spots[:, None]
    order = jnp.sum(jnp.where(hit, slots[None, :], 0), 1)
    reads = jnp.sum(jnp.where(hit, source[None, :] + 1, 0), 1)
    hit_unit = place[None, :] == spots[::UNIT][:, None]
    found = jnp.sum(jnp.where(hit_unit, local[None, :] + 1, 0), 1)
    writes = jnp.where(found > 0, found - 1, DUMMY)
    return jnp.stack(bounds), order, reads, writes


def load(tiles, *after):
    parts = 8
    size = tiles.shape[0] // parts

    def kernel(tile_ref, *refs):
        out, done, sem = refs[len(after) :]
        copies = [
            pltpu.make_async_copy(tile_ref.at[pl.ds(k * size, size)], out.at[pl.ds(k * size, size)], sem.at[k])
            for k in range(parts)
        ]
        for copy in copies:
            copy.start()
        done[...] = jnp.zeros_like(done)
        for copy in copies:
            copy.wait()

    return pl.pallas_call(
        kernel,
        in_specs=[pl.BlockSpec(memory_space=pltpu.HBM)] + [pl.BlockSpec(memory_space=pl.ANY)] * len(after),
        out_specs=[pl.BlockSpec(memory_space=pltpu.VMEM)] * 2,
        out_shape=[pltpu.VMEM(tiles.shape, tiles.dtype), jax.ShapeDtypeStruct((8, 128), jnp.int32)],
        scratch_shapes=[pltpu.SemaphoreType.DMA((parts,))],
        compiler_params=pltpu.CompilerParams(vmem_limit_bytes=1 << 20),
        cost_estimate=pl.CostEstimate(flops=0, bytes_accessed=25 << 20, transcendentals=0),
        name="load_tiles",
    )(pltpu.with_memory_space_constraint(tiles, pltpu.HBM), *after)


def assemble(pieces):
    total = BLK + sum(piece.shape[0] for piece in pieces)

    def kernel(*refs):
        fill_slab(refs[-1], [(ref, 0, ref.shape[0]) for ref in refs[:-1]])

    vmem = pl.BlockSpec(memory_space=pltpu.VMEM)
    return pl.pallas_call(
        kernel,
        in_specs=[vmem] * len(pieces),
        out_specs=vmem,
        out_shape=pltpu.VMEM((total, pieces[0].shape[1]), BF),
        compiler_params=pltpu.CompilerParams(vmem_limit_bytes=8 << 20),
        name="assemble",
    )(*pieces)


def cut(one, three, *after):
    half = one.shape[0] // 2

    def kernel(one_ref, three_ref, *refs):
        first, second = refs[-2:]
        first[...] = one_ref[pl.ds(0, half)]
        second[...] = three_ref[pl.ds(half, half)]

    vmem = pl.BlockSpec(memory_space=pltpu.VMEM)
    return pl.pallas_call(
        kernel,
        in_specs=[vmem, vmem] + [pl.BlockSpec(memory_space=pl.ANY)] * len(after),
        out_specs=[vmem] * 2,
        out_shape=[shape(half)] * 2,
        compiler_params=pltpu.CompilerParams(vmem_limit_bytes=8 << 20),
        name="cut",
    )(one, three, *after)


def relay(values, after):
    n = len(values)

    def kernel(*refs):
        for k in range(n):
            refs[n + 1 + k][...] = refs[k][...]

    vmem = pl.BlockSpec(memory_space=pltpu.VMEM)
    return pl.pallas_call(
        kernel,
        in_specs=[vmem] * n + [pl.BlockSpec(memory_space=pl.ANY)],
        out_specs=[vmem] * n,
        out_shape=[shape(value.shape[0]) for value in values],
        compiler_params=pltpu.CompilerParams(vmem_limit_bytes=8 << 20),
        name="relay",
    )(*values, after)


def fill_slab(slab, pieces):
    slab[pl.ds(0, BLK)] = jnp.zeros((BLK, slab.shape[1]), BF)
    place = BLK
    for ref, row, rows in pieces:
        slab[pl.ds(place, rows)] = ref[pl.ds(row, rows)]
        place += rows


def aggregate(name, step, lists, pieces, tiles, outs, flipped, start=None, mark=False):
    whole = len(pieces) == 1
    n_pieces = len(pieces)
    total = pieces[0][2] if whole else BLK + sum(rows for _, _, rows in pieces)
    blocks = max(first + size for first, size, _ in outs)

    def kernel(bounds, order, reads, writes, *refs):
        source = refs[:n_pieces]
        held = refs[n_pieces]
        refs = refs[n_pieces + 1 :]
        if start is not None:
            start_ref, refs = refs[0], refs[1:]
        out_refs, refs = refs[: len(outs)], refs[len(outs) :]
        if mark:
            refs[0][...] = jnp.zeros_like(refs[0])
            refs = refs[1:]
        acc = refs[0]
        if whole:
            slab = source[0]
        else:
            slab = refs[1]
            fill_slab(slab, [(ref, row, rows) for ref, (_, row, rows) in zip(source, pieces)])

        @pl.loop(0, blocks)
        def _(block):
            rows = pl.ds(pl.multiple_of(block * BLK, BLK), BLK)
            acc[rows] = jnp.zeros((BLK, acc.shape[1]), F32) if start is None else start_ref[rows]

        @pl.loop(bounds[step], bounds[step + 1])
        def _(group):
            for unit in range(UNROLL):
                spots = [group * GROUP + unit * UNIT + k for k in range(UNIT)]
                matrix = [held[order[spot]] for spot in spots]
                read = [slab[pl.ds(pl.multiple_of(reads[spot] * BLK, BLK), BLK)] for spot in spots]
                to = pl.ds(pl.multiple_of(writes[group * UNROLL + unit] * BLK, BLK), BLK)
                if flipped:
                    dims = (((0,), (0,)), ((), ()))
                    value = lax.dot_general(
                        jnp.concatenate(matrix, 0), jnp.concatenate(read, 0), dims, preferred_element_type=F32
                    )
                else:
                    value = jnp.dot(jnp.concatenate(matrix, 1), jnp.concatenate(read, 0), preferred_element_type=F32)
                acc[to] += value

        for out, (block, size, _) in zip(out_refs, outs):

            @pl.loop(0, size)
            def _(k, out=out, block=block):
                rows = pl.ds(pl.multiple_of((block + k) * BLK, BLK), BLK)
                out[pl.ds(pl.multiple_of(k * BLK, BLK), BLK)] = acc[rows].astype(out.dtype)

    smem = pl.BlockSpec(memory_space=pltpu.SMEM)
    vmem = pl.BlockSpec(memory_space=pltpu.VMEM)
    width = pieces[0][0].shape[1]
    extra = [] if start is None else [start]
    scratch = [pltpu.VMEM(((DUMMY + 1) * BLK, width), F32)]
    if not whole:
        scratch.append(pltpu.VMEM((total, width), BF))
    return pl.pallas_call(
        kernel,
        in_specs=[smem] * 4 + [vmem] * (n_pieces + 1 + len(extra)),
        out_specs=[vmem] * (len(outs) + mark),
        out_shape=[jax.ShapeDtypeStruct((size * BLK, width), dtype) for _, size, dtype in outs]
        + [jax.ShapeDtypeStruct((8, 128), jnp.int32)] * mark,
        scratch_shapes=scratch,
        compiler_params=pltpu.CompilerParams(vmem_limit_bytes=24 << 20),
        cost_estimate=pl.CostEstimate(flops=3 * 10**9, bytes_accessed=12 << 20, transcendentals=0),
        name=name,
    )(*lists, *[array for array, _, _ in pieces], pltpu.with_memory_space_constraint(tiles, pltpu.VMEM), *extra)


def local(name, body, out_shape, *operands):
    vmem = pl.BlockSpec(memory_space=pltpu.VMEM)
    return pl.pallas_call(
        body,
        in_specs=[vmem] * len(operands),
        out_specs=[vmem] * len(out_shape),
        out_shape=out_shape,
        compiler_params=pltpu.CompilerParams(vmem_limit_bytes=24 << 20),
        name=name,
    )(*operands)


def shape(rows, dtype=BF, width=256):
    return jax.ShapeDtypeStruct((rows, width), dtype)


def second_phase(*refs):
    ins, outs = refs[:8], refs[8:]
    for k in range(2):
        kept, one, three, two = ins[4 * k : 4 * k + 4]
        total = (kept[...] + two[...].astype(F32)) + (one[...].astype(F32) + three[...].astype(F32))
        for away, out in enumerate(outs[4 * k : 4 * k + 4]):
            out[...] = total[256 * away : 256 * away + 256].astype(out.dtype)


SCALE = math.sqrt(2.0 / math.pi)


def dense(*refs):
    sums, (cotangent, weight, activated, message_a, message_b) = refs[:8], refs[8:]
    matrix = weight[...]
    halves = []
    for k in range(2):
        kept, one, three, two = sums[4 * k : 4 * k + 4]
        halves.append((kept[...] + two[...].astype(F32)) + (one[...].astype(F32) + three[...].astype(F32)))
    aggregated = jnp.concatenate(halves, 0).astype(BF)
    pre = jnp.dot(aggregated, matrix, preferred_element_type=F32)
    square = pre * pre
    curve = jnp.tanh(SCALE * (pre + 0.044715 * (pre * square)))
    activated[...] = (0.5 * pre * (1.0 + curve)).astype(BF)
    slope = 0.5 * (1.0 + curve) + 0.5 * pre * (1.0 - curve * curve) * (SCALE * (1.0 + 3.0 * 0.044715 * square))
    grad_pre = (cotangent[...].astype(F32) * slope).astype(BF)
    mixed = lax.dot_general(grad_pre, matrix, (((1,), (1,)), ((), ())), preferred_element_type=F32).astype(BF)
    grad = lax.dot_general(aggregated, grad_pre, (((0,), (0,)), ((), ())), preferred_element_type=F32).astype(BF)
    for k, message in enumerate((message_a, message_b)):
        for half in range(2):
            message[pl.ds(half * 192, BLK)] = mixed[(2 * k + half) * BLK : (2 * k + half + 1) * BLK]
            message[pl.ds(half * 192 + BLK, 64)] = grad[(2 * k + half) * 64 : (2 * k + half + 1) * 64]


def four(zero, one, two, three):
    return (zero.astype(F32) + two.astype(F32)) + (one.astype(F32) + three.astype(F32))


def gathered(own, one, three, two, out):
    for half in range(2):
        for slot, ref in enumerate((own, one, three, two)):
            out[pl.ds(half * 576 + slot * BLK, BLK)] = ref[pl.ds(192 * half, BLK)]
        parts = [ref[pl.ds(192 * half + BLK, 64)] for ref in (own, one, two, three)]
        out[pl.ds(half * 576 + 512, 64)] = four(*parts).astype(BF)


def sum_ring(*refs):
    out = refs[-1]
    for k in range(2):
        own, one, three, *two = refs[5 * k : 5 * k + 5]
        for half in range(2):
            rows = pl.ds(576 * half + 512, 64)
            total = four(own[rows], one[rows], two[half][pl.ds(512, 64)], three[rows])
            out[pl.ds((2 * k + half) * 64, 64)] = total


def last_phase(own, received, grad, grad_received, by_one, by_two, late_two, late_one, kept):
    total = own[...] + received[...].astype(F32)
    by_one[pl.ds(0, 512)] = total[0:512].astype(BF)
    by_two[pl.ds(0, 512)] = total[512:1024].astype(BF)
    late_two[...] = total[1024:1280].astype(BF)
    late_one[...] = total[1280:1536].astype(BF)
    kept[...] = total[1536:2048]
    both = (grad[...] + grad_received[...]).astype(BF)
    by_one[pl.ds(512, 256)] = both
    by_two[pl.ds(512, 256)] = both


def last_forward(late_two, by_one, late_one, by_two, out_two, out_one):
    out_two[pl.ds(0, 256)] = (late_two[...].astype(F32) + by_one[pl.ds(0, 256)].astype(F32)).astype(BF)
    out_two[pl.ds(256, 128)] = by_one[pl.ds(512, 128)]
    out_one[pl.ds(0, 256)] = (late_one[...].astype(F32) + by_two[pl.ds(0, 256)].astype(F32)).astype(BF)
    out_one[pl.ds(256, 128)] = by_two[pl.ds(640, 128)]


def last_sum(kept, by_one, by_two, late_two, late_one, own_message, features, weight):
    first = kept[pl.ds(0, 256)] + (by_one[pl.ds(256, 256)].astype(F32) + late_two[pl.ds(0, 256)].astype(F32))
    second = kept[pl.ds(256, 256)] + (by_two[pl.ds(256, 256)].astype(F32) + late_one[pl.ds(0, 256)].astype(F32))
    features[pl.ds(0, 256)] = first.astype(BF)
    features[pl.ds(256, 256)] = second.astype(BF)
    for half, late in enumerate((late_two, late_one)):
        rows = pl.ds(512 + 128 * half, 128)
        weight[pl.ds(128 * half, 128)] = four(own_message[rows], by_one[rows], late[pl.ds(256, 128)], by_two[rows])


def per_device(features, weight, cotangent, tile_values, tile_rows, tile_cols, tile_count):
    tiles = tile_values[0, 0]
    near_one, near_two = swap(features, "x", ONE), swap(features, "x", TWO)
    across = swap_core(features)
    rows, cols = tile_rows[0, 0], tile_cols[0, 0]
    live = jnp.arange(rows.shape[0], dtype=jnp.int32) < tile_count[0, 0]
    row, col = lax.axis_index("row"), lax.axis_index("col")
    x, core, y, z = row // 2, row % 2, col // 4, col % 4

    sub = rows % 4
    y_away, z_away = distance(y, rows // 16), distance(z, rows // 4 % 4)
    second = sub >= 2
    half = sub % 2
    ring_one, ring_two = jnp.where(second, y_away, z_away), jnp.where(second, z_away, y_away)
    within = ring_two * 2 + half
    base = pick(ring_one, (48, 16, 0, 24))
    forward_key = base + jnp.where(second, jnp.where(ring_one % 2 == 1, 16, 8), 0) + within
    x_away, other = distance(x, cols // 8), (cols // 4 % 2) ^ core
    slot = x_away ^ (x_away >> 1)
    forward_source = other * 16 + slot * 4 + cols % 4
    far = ring_one == 2
    near_slot = ring_one ^ (ring_one >> 1)
    inner = ring_two ^ (ring_two >> 1)
    backward_source = jnp.where(far, second * 8, second * 24 + near_slot * 8) + half * 4 + inner
    backward_role = pick(cols % 4 // 2 * 4 + x_away, ROLE)
    backward_key = jnp.where(far, 32, 0) + (1 - other) * 16 + backward_role * 2 + cols % 2

    forward = plan(forward_key, forward_source, live, ((0, 16), (16, 48), (48, 64)))

    far_first, far_second = cut(near_one, near_two, *forward)
    held_tiles, loaded = load(tiles, far_first)
    far_first, far_second = swap(far_first, "x", TWO), swap(far_second, "x", ONE)
    far_first, far_second = relay((far_first, far_second), loaded)
    across_near = [swap_core(near_one), swap_core(near_two)]
    across_far = [swap_core(far_first), swap_core(far_second)]
    held = [features, near_one, near_two, far_first, far_second, across, *across_near, *across_far]
    slab = assemble(held)
    pieces = [(slab, 0, slab.shape[0])]

    def ways(axis, one, three, two):
        return swap(one, axis, ONE), swap(three, axis, TWO), swap(two, axis, FAR)

    def out(*dtypes):
        return [(8 * k, 8, dtype) for k, dtype in enumerate(dtypes)]

    a_two, b_two = aggregate("forward_far", 0, forward, pieces, held_tiles, out(BF, BF), False)
    a_two, b_two = swap(a_two, "z", FAR), swap(b_two, "y", FAR)
    a_one, a_three, b_one, b_three = aggregate(
        "forward_near", 1, forward, pieces, held_tiles, out(BF, BF, BF, BF), False
    )
    a_one, a_three = swap(a_one, "z", ONE), swap(a_three, "z", TWO)
    b_one, b_three = swap(b_one, "y", ONE), swap(b_three, "y", TWO)
    a_own, b_own, after = aggregate("forward_own", 2, forward, pieces, held_tiles, out(F32, F32), False, None, True)
    backward = plan(
        backward_key + after[0, 0], backward_source + after[0, 0], live, ((0, 32), (32, 48), (48, 64))
    )
    second_shapes = [shape(256, F32), shape(256), shape(256), shape(256)]
    a_own, a_one, a_two, a_three, b_own, b_one, b_two, b_three = local(
        "second_phase", second_phase, second_shapes * 2,
        a_own, a_one, a_three, a_two, b_own, b_one, b_three, b_two,
    )
    a_sums = [a_own, *ways("y", a_one, a_three, a_two)]
    b_sums = [b_own, *ways("z", b_one, b_three, b_two)]
    activated, a_own, b_own = local(
        "dense", dense, [shape(512), shape(384), shape(384)], *a_sums, *b_sums, cotangent, weight
    )

    a_held = [a_own, *ways("y", a_own, a_own, a_own)]
    b_held = [b_own, *ways("z", b_own, b_own, b_own)]
    (a_own,) = local("gathered_a", gathered, [shape(1152)], *a_held)
    a_one, a_three = swap(a_own, "z", ONE), swap(a_own, "z", TWO)
    (b_own,) = local("gathered_b", gathered, [shape(1152)], *b_held)
    b_one, b_three = swap(b_own, "y", ONE), swap(b_own, "y", TWO)
    again, loaded = load(tiles, a_own, b_own)
    a_first, a_second = cut(a_one, a_three, loaded)
    b_first, b_second = cut(b_one, b_three, loaded)
    a_far = swap(a_first, "z", TWO), swap(a_second, "z", ONE)
    b_far = swap(b_first, "y", TWO), swap(b_second, "y", ONE)

    near = [
        (piece, row, 512) for piece in (a_own, a_one, a_three, b_own, b_one, b_three) for row in (0, 576)
    ]
    distant = [(piece, 0, 512) for piece in (*a_far, *b_far)]
    other_start, own_start = aggregate(
        "backward_near", 0, backward, near, again, [(0, 16, F32), (16, 16, F32)], True
    )
    (other_sum,) = aggregate("backward_other", 1, backward, distant, again, [(0, 16, BF)], True, other_start)
    received = swap_core(other_sum)
    (grad,) = local(
        "sum_ring", sum_ring, [shape(256, F32)], a_own, a_one, a_three, *a_far, b_own, b_one, b_three, *b_far
    )
    grad_received = swap_core(grad)
    (own_sum,) = aggregate("backward_own", 2, backward, distant, again, [(0, 16, F32)], True, own_start)
    by_one, by_two, late_two, late_one, kept = local(
        "last_phase", last_phase, [shape(768), shape(768), shape(256), shape(256), shape(512, F32)],
        own_sum, received, grad, grad_received,
    )
    got_one, got_two = swap(by_one, "x", ONE), swap(by_two, "x", TWO)
    late_two, late_one = local(
        "last_forward", last_forward, [shape(384), shape(384)], late_two, got_one, late_one, got_two
    )
    late_two, late_one = swap(late_two, "x", TWO), swap(late_one, "x", ONE)
    grad_features, grad_weight = local(
        "last_sum", last_sum, [shape(512), shape(256, F32)], kept, got_one, got_two, late_two, late_one, by_one
    )
    return activated, grad_features, grad_weight


def solution(mesh):
    in_specs = (
        P(("row", "col"), None),
        P(),
        P(("row", "col"), None),
        P("row", "col", None, None, None),
        P("row", "col", None),
        P("row", "col", None),
        P("row", "col"),
    )
    out_specs = (P(("row", "col"), None), P(("row", "col"), None), P())
    return jax.shard_map(
        per_device, mesh=mesh, in_specs=in_specs, out_specs=out_specs, check_vma=False
    )
```

```python
import math

import jax
import jax.numpy as jnp
from jax import lax
from jax.experimental import pallas as pl
from jax.experimental.pallas import tpu as pltpu
from jax.sharding import PartitionSpec as P

BF = jnp.bfloat16
F32 = jnp.float32
BLK = 128
UNIT = 2
UNROLL = 8
GROUP = UNIT * UNROLL
KEYS = 64
DUMMY = 32

ONE = ((0, 1), (1, 0), (2, 3), (3, 2))
TWO = ((1, 2), (2, 1), (3, 0), (0, 3))
FAR = ((0, 2), (2, 0), (1, 3), (3, 1))


def swap(value, axis, pairs):
    if axis == "z":
        return lax.ppermute(value, "col", [(y * 4 + a, y * 4 + b) for y in range(4) for a, b in pairs])
    if axis == "y":
        return lax.ppermute(value, "col", [(a * 4 + z, b * 4 + z) for z in range(4) for a, b in pairs])
    return lax.ppermute(value, "row", [(a * 2 + k, b * 2 + k) for k in range(2) for a, b in pairs])


def swap_core(value):
    return lax.ppermute(value, "row", [(2 * x + k, 2 * x + 1 - k) for x in range(4) for k in range(2)])


def distance(here, there):
    return ((1 - 2 * (here & 1)) * (there - here)) & 3


def pick(index, table):
    found = jnp.zeros_like(index)
    for place, entry in enumerate(table):
        found = jnp.where(index == place, entry, found)
    return found


ROLE = (6, 1, 0, 4, 7, 5, 2, 3)


FORWARD = ((0, 8), (8, 16), (16, 32), (32, 48), (48, 64))
BACKWARD = ((0, 32), (32, 48), (48, 64))
ROOM = 640


def sort_tiles(out, keys, source, live, segments):
    total = keys.shape[1]

    def iota(rows, lanes, axis):
        return lax.broadcasted_iota(jnp.int32, (rows, lanes), axis).astype(F32)

    def column(value):
        return jnp.transpose(jnp.broadcast_to(value, (128, total)))

    def segment_of(key):
        return sum((key >= first).astype(F32) for first, _ in segments) - 1.0

    local = keys
    for first, _ in segments[1:]:
        local = jnp.where(keys >= first, keys - first, local)
    slots = lax.broadcasted_iota(jnp.int32, (1, total), 1)
    payload = (slots + 512 * (source + 1) + 65536 * (local + 1)).astype(F32)
    keys = jnp.where(live, keys, KEYS).astype(F32)
    key_column = column(keys)
    lane = iota(1, 128, 1)
    count = jnp.sum(jnp.where(key_column == lane, 1.0, 0.0), 0, keepdims=True)
    padded = jnp.where(lane < KEYS, ((count.astype(jnp.int32) + 1) >> 1 << 1).astype(F32), 0.0)
    bounds = [jnp.zeros((1, 1), F32)]
    for index in range(len(segments)):
        size = jnp.sum(jnp.where(segment_of(lane) == index, padded, 0.0), 1, keepdims=True).astype(jnp.int32)
        bounds.append(bounds[-1] + ((size + GROUP - 1) // GROUP).astype(F32))
    key, before = iota(KEYS, 128, 0), iota(KEYS, 128, 1)
    counted = (before < key) & (segment_of(before) == segment_of(key))
    offset = jnp.sum(jnp.where(counted, padded, 0.0), 1, keepdims=True)
    for index in range(len(segments)):
        offset += jnp.where(segment_of(key[:, :1]) == index, GROUP * bounds[index], 0.0)
    same = jnp.concatenate([key_column] * (total // 128), 1) == keys
    rank = jnp.sum(jnp.where(same & (iota(total, total, 0) < iota(total, total, 1)), 1.0, 0.0), 0, keepdims=True)
    start = jnp.sum(jnp.where(iota(KEYS, total, 0) == keys, offset, 0.0), 0, keepdims=True)
    place_column = column(jnp.where(live, rank + start, -1.0))
    payload_column = column(payload)
    for block in range(ROOM // 128):
        here = pl.ds(block * 128, 128)
        found = jnp.sum(jnp.where(place_column == lane + 128.0 * block, payload_column, 0.0), 0, keepdims=True)
        found = found.astype(jnp.int32)
        out[0:1, here] = found & 511
        out[1:2, here] = (found >> 9) & 127
        out[2:3, here] = jnp.where(found == 0, DUMMY, (found >> 16) - 1)
        out[3:4, here] = sum(jnp.where(lane >= index, bounds[index] - bounds[index - 1], 0.0) for index in range(1, len(bounds))).astype(jnp.int32)


def plan(position, count, rows, cols):
    def kernel(position_ref, count_ref, rows_ref, cols_ref, forward, backward):
        x, core, y, z = [position_ref[k] for k in range(4)]
        rows, cols = rows_ref[...], cols_ref[...]
        live = lax.broadcasted_iota(jnp.int32, rows.shape, 1) < count_ref[0, 0]
        y_away, z_away = distance(y, rows >> 4), distance(z, (rows >> 2) & 3)
        second = (rows & 2) != 0
        half = rows & 1
        ring_one, ring_two = jnp.where(second, y_away, z_away), jnp.where(second, z_away, y_away)
        base = jnp.where(second, pick(ring_one, (56, 16, 8, 24)), pick(ring_one, (48, 32, 0, 40)))
        x_away, other = distance(x, cols >> 3), ((cols >> 2) & 1) ^ core
        slot = x_away ^ (x_away >> 1)
        source = other * 16 + slot * 4 + (cols & 3)
        sort_tiles(forward, base + ring_two * 2 + half, source, live, FORWARD)
        far = ring_one == 2
        near_slot = ring_one ^ (ring_one >> 1)
        inner = ring_two ^ (ring_two >> 1)
        source = jnp.where(second, jnp.where(far, 8, 24 + near_slot * 8), jnp.where(far, 0, near_slot * 8))
        source += half * 4 + inner
        role = pick(((cols >> 1) & 1) * 4 + x_away, ROLE)
        keys = jnp.where(far, 32, 0) + (1 - other) * 16 + role * 2 + (cols & 1)
        sort_tiles(backward, keys, source, live, BACKWARD)

    smem = pl.BlockSpec(memory_space=pltpu.SMEM)
    vmem = pl.BlockSpec(memory_space=pltpu.VMEM)
    return pl.pallas_call(
        kernel,
        in_specs=[smem, smem, vmem, vmem],
        out_specs=[vmem] * 2,
        out_shape=[jax.ShapeDtypeStruct((4, ROOM), jnp.int32)] * 2,
        compiler_params=pltpu.CompilerParams(vmem_limit_bytes=8 << 20),
        name="plan",
    )(position, count, rows, cols)


def load(tiles, *after):
    parts = 8
    size = tiles.shape[0] // parts

    def kernel(tile_ref, *refs):
        out, done, sem = refs[len(after) :]
        copies = [
            pltpu.make_async_copy(tile_ref.at[pl.ds(k * size, size)], out.at[pl.ds(k * size, size)], sem.at[k])
            for k in range(parts)
        ]
        for copy in copies:
            copy.start()
        done[...] = jnp.zeros_like(done)
        for copy in copies:
            copy.wait()

    return pl.pallas_call(
        kernel,
        in_specs=[pl.BlockSpec(memory_space=pltpu.HBM)] + [pl.BlockSpec(memory_space=pl.ANY)] * len(after),
        out_specs=[pl.BlockSpec(memory_space=pltpu.VMEM)] * 2,
        out_shape=[pltpu.VMEM(tiles.shape, tiles.dtype), jax.ShapeDtypeStruct((8, 128), jnp.int32)],
        scratch_shapes=[pltpu.SemaphoreType.DMA((parts,))],
        compiler_params=pltpu.CompilerParams(vmem_limit_bytes=1 << 20),
        cost_estimate=pl.CostEstimate(flops=0, bytes_accessed=25 << 20, transcendentals=0),
        name="load_tiles",
    )(pltpu.with_memory_space_constraint(tiles, pltpu.HBM), *after)


def assemble(pieces):
    total = BLK + sum(piece.shape[0] for piece in pieces)

    def kernel(*refs):
        fill_slab(refs[-1], [(ref, 0, ref.shape[0]) for ref in refs[:-1]])

    vmem = pl.BlockSpec(memory_space=pltpu.VMEM)
    return pl.pallas_call(
        kernel,
        in_specs=[vmem] * len(pieces),
        out_specs=vmem,
        out_shape=pltpu.VMEM((total, pieces[0].shape[1]), BF),
        compiler_params=pltpu.CompilerParams(vmem_limit_bytes=8 << 20),
        name="assemble",
    )(*pieces)


def cut(one, three, *after):
    half = one.shape[0] // 2

    def kernel(one_ref, three_ref, *refs):
        first, second = refs[-2:]
        first[...] = one_ref[pl.ds(0, half)]
        second[...] = three_ref[pl.ds(half, half)]

    vmem = pl.BlockSpec(memory_space=pltpu.VMEM)
    return pl.pallas_call(
        kernel,
        in_specs=[vmem, vmem] + [pl.BlockSpec(memory_space=pl.ANY)] * len(after),
        out_specs=[vmem] * 2,
        out_shape=[shape(half)] * 2,
        compiler_params=pltpu.CompilerParams(vmem_limit_bytes=8 << 20),
        name="cut",
    )(one, three, *after)


def relay(values, after):
    n = len(values)

    def kernel(*refs):
        for k in range(n):
            refs[n + 1 + k][...] = refs[k][...]

    vmem = pl.BlockSpec(memory_space=pltpu.VMEM)
    return pl.pallas_call(
        kernel,
        in_specs=[vmem] * n + [pl.BlockSpec(memory_space=pl.ANY)],
        out_specs=[vmem] * n,
        out_shape=[shape(value.shape[0]) for value in values],
        compiler_params=pltpu.CompilerParams(vmem_limit_bytes=8 << 20),
        name="relay",
    )(*values, after)


def fill_slab(slab, pieces):
    slab[pl.ds(0, BLK)] = jnp.zeros((BLK, slab.shape[1]), BF)
    place = BLK
    for ref, row, rows in pieces:
        slab[pl.ds(place, rows)] = ref[pl.ds(row, rows)]
        place += rows


def aggregate(name, step, lists, pieces, tiles, outs, flipped, start=None):
    whole = len(pieces) == 1
    n_pieces = len(pieces)
    total = pieces[0][2] if whole else BLK + sum(rows for _, _, rows in pieces)
    blocks = max(first + size for first, size, _ in outs)

    def kernel(listed, *refs):
        source = refs[:n_pieces]
        held = refs[n_pieces]
        refs = refs[n_pieces + 1 :]
        if start is not None:
            start_ref, refs = refs[0], refs[1:]
        out_refs, refs = refs[: len(outs)], refs[len(outs) :]
        acc = refs[0]
        if whole:
            slab = source[0]
        else:
            slab = refs[1]
            fill_slab(slab, [(ref, row, rows) for ref, (_, row, rows) in zip(source, pieces)])

        @pl.loop(0, blocks)
        def _(block):
            rows = pl.ds(pl.multiple_of(block * BLK, BLK), BLK)
            acc[rows] = jnp.zeros((BLK, acc.shape[1]), F32) if start is None else start_ref[rows]

        @pl.loop(listed[3, step], listed[3, step + 1])
        def _(group):
            for unit in range(UNROLL):
                spots = [group * GROUP + unit * UNIT + k for k in range(UNIT)]
                matrix = [held[listed[0, spot]] for spot in spots]
                read = [slab[pl.ds(pl.multiple_of(listed[1, spot] * BLK, BLK), BLK)] for spot in spots]
                to = pl.ds(pl.multiple_of(listed[2, spots[0]] * BLK, BLK), BLK)
                if flipped:
                    dims = (((0,), (0,)), ((), ()))
                    value = lax.dot_general(
                        jnp.concatenate(matrix, 0), jnp.concatenate(read, 0), dims, preferred_element_type=F32
                    )
                else:
                    value = jnp.dot(jnp.concatenate(matrix, 1), jnp.concatenate(read, 0), preferred_element_type=F32)
                acc[to] += value

        for out, (block, size, _) in zip(out_refs, outs):

            @pl.loop(0, size)
            def _(k, out=out, block=block):
                rows = pl.ds(pl.multiple_of((block + k) * BLK, BLK), BLK)
                out[pl.ds(pl.multiple_of(k * BLK, BLK), BLK)] = acc[rows].astype(out.dtype)

    smem = pl.BlockSpec(memory_space=pltpu.SMEM)
    vmem = pl.BlockSpec(memory_space=pltpu.VMEM)
    width = pieces[0][0].shape[1]
    extra = [] if start is None else [start]
    scratch = [pltpu.VMEM(((DUMMY + 1) * BLK, width), F32)]
    if not whole:
        scratch.append(pltpu.VMEM((total, width), BF))
    return pl.pallas_call(
        kernel,
        in_specs=[smem] + [vmem] * (n_pieces + 1 + len(extra)),
        out_specs=[vmem] * len(outs),
        out_shape=[jax.ShapeDtypeStruct((size * BLK, width), dtype) for _, size, dtype in outs],
        scratch_shapes=scratch,
        compiler_params=pltpu.CompilerParams(vmem_limit_bytes=24 << 20),
        cost_estimate=pl.CostEstimate(flops=10**6, bytes_accessed=1 << 17, transcendentals=0),
        name=name,
    )(lists, *[array for array, _, _ in pieces], pltpu.with_memory_space_constraint(tiles, pltpu.VMEM), *extra)


def local(name, body, out_shape, *operands):
    vmem = pl.BlockSpec(memory_space=pltpu.VMEM)
    return pl.pallas_call(
        body,
        in_specs=[vmem] * len(operands),
        out_specs=[vmem] * len(out_shape),
        out_shape=out_shape,
        compiler_params=pltpu.CompilerParams(vmem_limit_bytes=24 << 20),
        name=name,
    )(*operands)


def shape(rows, dtype=BF, width=256):
    return jax.ShapeDtypeStruct((rows, width), dtype)


def second_phase(*refs):
    ins, outs = refs[:8], refs[8:]
    for k in range(2):
        kept, one, three, two = ins[4 * k : 4 * k + 4]
        total = (kept[...] + two[...].astype(F32)) + (one[...].astype(F32) + three[...].astype(F32))
        for away, out in enumerate(outs[4 * k : 4 * k + 4]):
            out[...] = total[256 * away : 256 * away + 256].astype(out.dtype)


SCALE = math.sqrt(2.0 / math.pi)


def dense(*refs):
    sums, (cotangent, weight, activated, message_a, message_b) = refs[:8], refs[8:]
    matrix = weight[...]
    halves = []
    for k in range(2):
        kept, one, three, two = sums[4 * k : 4 * k + 4]
        halves.append((kept[...] + two[...].astype(F32)) + (one[...].astype(F32) + three[...].astype(F32)))
    aggregated = jnp.concatenate(halves, 0).astype(BF)
    pre = jnp.dot(aggregated, matrix, preferred_element_type=F32)
    square = pre * pre
    curve = jnp.tanh(SCALE * (pre + 0.044715 * (pre * square)))
    activated[...] = (0.5 * pre * (1.0 + curve)).astype(BF)
    slope = 0.5 * (1.0 + curve) + 0.5 * pre * (1.0 - curve * curve) * (SCALE * (1.0 + 3.0 * 0.044715 * square))
    grad_pre = (cotangent[...].astype(F32) * slope).astype(BF)
    mixed = lax.dot_general(grad_pre, matrix, (((1,), (1,)), ((), ())), preferred_element_type=F32).astype(BF)
    grad = lax.dot_general(aggregated, grad_pre, (((0,), (0,)), ((), ())), preferred_element_type=F32).astype(BF)
    for k, message in enumerate((message_a, message_b)):
        for half in range(2):
            message[pl.ds(half * 192, BLK)] = mixed[(2 * k + half) * BLK : (2 * k + half + 1) * BLK]
            message[pl.ds(half * 192 + BLK, 64)] = grad[(2 * k + half) * 64 : (2 * k + half + 1) * 64]


def four(zero, one, two, three):
    return (zero.astype(F32) + two.astype(F32)) + (one.astype(F32) + three.astype(F32))


def gathered(own, one, three, two, out):
    for half in range(2):
        for slot, ref in enumerate((own, one, three, two)):
            out[pl.ds(half * 576 + slot * BLK, BLK)] = ref[pl.ds(192 * half, BLK)]
        parts = [ref[pl.ds(192 * half + BLK, 64)] for ref in (own, one, two, three)]
        out[pl.ds(half * 576 + 512, 64)] = four(*parts).astype(BF)


def sum_ring(*refs):
    out = refs[-1]
    for k in range(2):
        own, one, three, *two = refs[5 * k : 5 * k + 5]
        for half in range(2):
            rows = pl.ds(576 * half + 512, 64)
            total = four(own[rows], one[rows], two[half][pl.ds(512, 64)], three[rows])
            out[pl.ds((2 * k + half) * 64, 64)] = total


def last_phase(own, received, grad, grad_received, by_one, by_two, late_two, late_one, kept):
    total = own[...] + received[...].astype(F32)
    by_one[pl.ds(0, 512)] = total[0:512].astype(BF)
    by_two[pl.ds(0, 512)] = total[512:1024].astype(BF)
    late_two[...] = total[1024:1280].astype(BF)
    late_one[...] = total[1280:1536].astype(BF)
    kept[...] = total[1536:2048]
    both = (grad[...] + grad_received[...]).astype(BF)
    by_one[pl.ds(512, 256)] = both
    by_two[pl.ds(512, 256)] = both


def last_forward(late_two, by_one, late_one, by_two, out_two, out_one):
    out_two[pl.ds(0, 256)] = (late_two[...].astype(F32) + by_one[pl.ds(0, 256)].astype(F32)).astype(BF)
    out_two[pl.ds(256, 128)] = by_one[pl.ds(512, 128)]
    out_one[pl.ds(0, 256)] = (late_one[...].astype(F32) + by_two[pl.ds(0, 256)].astype(F32)).astype(BF)
    out_one[pl.ds(256, 128)] = by_two[pl.ds(640, 128)]


def last_sum(kept, by_one, by_two, late_two, late_one, own_message, features, weight):
    first = kept[pl.ds(0, 256)] + (by_one[pl.ds(256, 256)].astype(F32) + late_two[pl.ds(0, 256)].astype(F32))
    second = kept[pl.ds(256, 256)] + (by_two[pl.ds(256, 256)].astype(F32) + late_one[pl.ds(0, 256)].astype(F32))
    features[pl.ds(0, 256)] = first.astype(BF)
    features[pl.ds(256, 256)] = second.astype(BF)
    for half, late in enumerate((late_two, late_one)):
        rows = pl.ds(512 + 128 * half, 128)
        weight[pl.ds(128 * half, 128)] = four(own_message[rows], by_one[rows], late[pl.ds(256, 128)], by_two[rows])


def per_device(features, weight, cotangent, tile_values, tile_rows, tile_cols, tile_count):
    tiles = tile_values[0, 0]
    near_one, near_two = swap(features, "x", ONE), swap(features, "x", TWO)
    across = swap_core(features)
    row, col = lax.axis_index("row"), lax.axis_index("col")
    position = jnp.stack([row // 2, row % 2, col // 4, col % 4]).astype(jnp.int32)
    forward, backward = plan(position, tile_count, tile_rows[0], tile_cols[0])

    far_away = swap(features, "x", FAR)
    held_tiles, loaded = load(tiles, forward, backward)
    (far_away,) = relay((far_away,), loaded)
    across_near = [swap_core(near_one), swap_core(near_two)]
    held = [features, near_one, near_two, far_away, across, *across_near, swap_core(far_away)]
    slab = assemble(held)
    pieces = [(slab, 0, slab.shape[0])]

    def ways(axis, one, three, two):
        return swap(one, axis, ONE), swap(three, axis, TWO), swap(two, axis, FAR)

    def out(*dtypes):
        return [(8 * k, 8, dtype) for k, dtype in enumerate(dtypes)]

    (a_two,) = aggregate("forward_far_a", 0, forward, pieces, held_tiles, out(BF), False)
    a_two = swap(a_two, "z", FAR)
    (b_two,) = aggregate("forward_far_b", 1, forward, pieces, held_tiles, out(BF), False)
    b_two = swap(b_two, "y", FAR)
    b_one, b_three = aggregate("forward_near_b", 2, forward, pieces, held_tiles, out(BF, BF), False)
    b_one, b_three = swap(b_one, "y", ONE), swap(b_three, "y", TWO)
    a_one, a_three = aggregate("forward_near_a", 3, forward, pieces, held_tiles, out(BF, BF), False)
    a_one, a_three = swap(a_one, "z", ONE), swap(a_three, "z", TWO)
    a_own, b_own = aggregate("forward_own", 4, forward, pieces, held_tiles, out(F32, F32), False)
    second_shapes = [shape(256, F32), shape(256), shape(256), shape(256)]
    a_own, a_one, a_two, a_three, b_own, b_one, b_two, b_three = local(
        "second_phase", second_phase, second_shapes * 2,
        a_own, a_one, a_three, a_two, b_own, b_one, b_three, b_two,
    )
    a_sums = [a_own, *ways("y", a_one, a_three, a_two)]
    b_sums = [b_own, *ways("z", b_one, b_three, b_two)]
    activated, a_own, b_own = local(
        "dense", dense, [shape(512), shape(384), shape(384)], *a_sums, *b_sums, cotangent, weight
    )

    a_held = [a_own, *ways("y", a_own, a_own, a_own)]
    b_held = [b_own, *ways("z", b_own, b_own, b_own)]
    (a_own,) = local("gathered_a", gathered, [shape(1152)], *a_held)
    a_one, a_three = swap(a_own, "z", ONE), swap(a_own, "z", TWO)
    (b_own,) = local("gathered_b", gathered, [shape(1152)], *b_held)
    b_one, b_three = swap(b_own, "y", ONE), swap(b_own, "y", TWO)
    again, loaded = load(tiles, a_own, b_own)
    a_first, a_second = cut(a_one, a_three, loaded)
    b_first, b_second = cut(b_one, b_three, loaded)
    a_far = swap(a_first, "z", TWO), swap(a_second, "z", ONE)
    b_far = swap(b_first, "y", TWO), swap(b_second, "y", ONE)

    near = [
        (piece, row, 512) for piece in (a_own, a_one, a_three, b_own, b_one, b_three) for row in (0, 576)
    ]
    distant = [(piece, 0, 512) for piece in (*a_far, *b_far)]
    other_start, own_start = aggregate(
        "backward_near", 0, backward, near, again, [(0, 16, F32), (16, 16, F32)], True
    )
    (other_sum,) = aggregate("backward_other", 1, backward, distant, again, [(0, 16, BF)], True, other_start)
    received = swap_core(other_sum)
    (grad,) = local(
        "sum_ring", sum_ring, [shape(256, F32)], a_own, a_one, a_three, *a_far, b_own, b_one, b_three, *b_far
    )
    grad_received = swap_core(grad)
    (own_sum,) = aggregate("backward_own", 2, backward, distant, again, [(0, 16, F32)], True, own_start)
    by_one, by_two, late_two, late_one, kept = local(
        "last_phase", last_phase, [shape(768), shape(768), shape(256), shape(256), shape(512, F32)],
        own_sum, received, grad, grad_received,
    )
    got_one, got_two = swap(by_one, "x", ONE), swap(by_two, "x", TWO)
    late_two, late_one = local(
        "last_forward", last_forward, [shape(384), shape(384)], late_two, got_one, late_one, got_two
    )
    late_two, late_one = swap(late_two, "x", TWO), swap(late_one, "x", ONE)
    grad_features, grad_weight = local(
        "last_sum", last_sum, [shape(512), shape(256, F32)], kept, got_one, got_two, late_two, late_one, by_one
    )
    return activated, grad_features, grad_weight


def solution(mesh):
    in_specs = (
        P(("row", "col"), None),
        P(),
        P(("row", "col"), None),
        P("row", "col", None, None, None),
        P("row", "col", None),
        P("row", "col", None),
        P("row", "col"),
    )
    out_specs = (P(("row", "col"), None), P(("row", "col"), None), P())
    return jax.shard_map(
        per_device, mesh=mesh, in_specs=in_specs, out_specs=out_specs, check_vma=False
    )
```

```python
import math

import jax
import jax.numpy as jnp
from jax import lax
from jax.experimental import pallas as pl
from jax.experimental.pallas import tpu as pltpu
from jax.sharding import PartitionSpec as P

BF = jnp.bfloat16
F32 = jnp.float32
BLK = 128
UNIT = 2
UNROLL = 8
GROUP = UNIT * UNROLL

ONE = ((0, 1), (1, 0), (2, 3), (3, 2))
TWO = ((1, 2), (2, 1), (3, 0), (0, 3))
FAR = ((0, 2), (2, 0), (1, 3), (3, 1))


def swap(value, axis, pairs):
    if axis == "z":
        return lax.ppermute(value, "col", [(y * 4 + a, y * 4 + b) for y in range(4) for a, b in pairs])
    if axis == "y":
        return lax.ppermute(value, "col", [(a * 4 + z, b * 4 + z) for z in range(4) for a, b in pairs])
    return lax.ppermute(value, "row", [(a * 2 + k, b * 2 + k) for k in range(2) for a, b in pairs])


def swap_core(value):
    return lax.ppermute(value, "row", [(2 * x + k, 2 * x + 1 - k) for x in range(4) for k in range(2)])


def distance(here, there):
    return ((1 - 2 * (here & 1)) * (there - here)) & 3


def pick(index, table):
    found = jnp.zeros_like(index)
    for place, entry in enumerate(table):
        found = jnp.where(index == place, entry, found)
    return found


FORWARD = ((0, 16), (16, 32), (32, 48), (48, 64))
BACKWARD = ((0, 32), (32, 64), (64, 80), (80, 96))
ROOM = 640


def sort_tiles(out, keys, source, live, segments):
    total, n_keys = keys.shape[1], segments[-1][1]

    def iota(rows, lanes, axis):
        return lax.broadcasted_iota(jnp.int32, (rows, lanes), axis).astype(F32)

    def column(value):
        return jnp.transpose(jnp.broadcast_to(value, (128, total)))

    def segment_of(key):
        return sum((key >= first).astype(F32) for first, _ in segments) - 1.0

    local = keys
    for first, _ in segments[1:]:
        local = jnp.where(keys >= first, keys - first, local)
    slots = lax.broadcasted_iota(jnp.int32, (1, total), 1)
    payload = (slots + 512 * (source + 1) + 65536 * (local + 1)).astype(F32)
    keys = jnp.where(live, keys, n_keys).astype(F32)
    key_column = column(keys)
    lane = iota(1, 128, 1)
    count = jnp.sum(jnp.where(key_column == lane, 1.0, 0.0), 0, keepdims=True)
    padded = jnp.where(lane < n_keys, ((count.astype(jnp.int32) + 1) >> 1 << 1).astype(F32), 0.0)
    bounds = [jnp.zeros((1, 1), F32)]
    for index in range(len(segments)):
        size = jnp.sum(jnp.where(segment_of(lane) == index, padded, 0.0), 1, keepdims=True).astype(jnp.int32)
        bounds.append(bounds[-1] + ((size + GROUP - 1) // GROUP).astype(F32))
    key, before = iota(n_keys, 128, 0), iota(n_keys, 128, 1)
    counted = (before < key) & (segment_of(before) == segment_of(key))
    offset = jnp.sum(jnp.where(counted, padded, 0.0), 1, keepdims=True)
    for index in range(len(segments)):
        offset += jnp.where(segment_of(key[:, :1]) == index, GROUP * bounds[index], 0.0)
    same = jnp.concatenate([key_column] * (total // 128), 1) == keys
    rank = jnp.sum(jnp.where(same & (iota(total, total, 0) < iota(total, total, 1)), 1.0, 0.0), 0, keepdims=True)
    start = jnp.sum(jnp.where(iota(n_keys, total, 0) == keys, offset, 0.0), 0, keepdims=True)
    place_column = column(jnp.where(live, rank + start, -1.0))
    payload_column = column(payload)
    for block in range(ROOM // 128):
        here = pl.ds(block * 128, 128)
        found = jnp.sum(jnp.where(place_column == lane + 128.0 * block, payload_column, 0.0), 0, keepdims=True)
        found = found.astype(jnp.int32)
        out[0:1, here] = found & 511
        out[1:2, here] = (found >> 9) & 127
        out[2:3, here] = jnp.where(found == 0, 0, (found >> 16) - 1)
        out[3:4, here] = sum(jnp.where(lane >= index, bounds[index] - bounds[index - 1], 0.0) for index in range(1, len(bounds))).astype(jnp.int32)


def plan(position, count, rows, cols):
    def kernel(position_ref, count_ref, rows_ref, cols_ref, forward, backward):
        x, core, y, z = [position_ref[k] for k in range(4)]
        rows, cols = rows_ref[...], cols_ref[...]
        live = lax.broadcasted_iota(jnp.int32, rows.shape, 1) < count_ref[0, 0]
        y_away, z_away = distance(y, rows >> 4), distance(z, (rows >> 2) & 3)
        second = (rows & 2) != 0
        half = rows & 1
        ring_one, ring_two = jnp.where(second, y_away, z_away), jnp.where(second, z_away, y_away)
        base = jnp.where(second, pick(ring_one, (56, 16, 8, 24)), pick(ring_one, (48, 32, 0, 40)))
        x_away, other = distance(x, cols >> 3), ((cols >> 2) & 1) ^ core
        slot = x_away ^ (x_away >> 1)
        source = other * 16 + slot * 4 + (cols & 3)
        sort_tiles(forward, base + ring_two * 2 + half, source, live, FORWARD)
        far = ring_one == 2
        near = ring_one % 2 == 1
        inner = ring_two ^ (ring_two >> 1)
        source = jnp.where(near, jnp.where(second, 16, 0) + (ring_one >> 1) * 8, jnp.where(second, 8, 0))
        source += half * 4 + inner
        keys = jnp.where(far, 64, jnp.where(near, 32, 0)) + (1 - other) * 16 + x_away * 4 + (cols & 3)
        sort_tiles(backward, keys, source, live, BACKWARD)

    smem = pl.BlockSpec(memory_space=pltpu.SMEM)
    vmem = pl.BlockSpec(memory_space=pltpu.VMEM)
    return pl.pallas_call(
        kernel,
        in_specs=[smem, smem, vmem, vmem],
        out_specs=[vmem] * 2,
        out_shape=[jax.ShapeDtypeStruct((4, ROOM), jnp.int32)] * 2,
        compiler_params=pltpu.CompilerParams(vmem_limit_bytes=8 << 20),
        name="plan",
    )(position, count, rows, cols)


def load(tiles, *after):
    parts = 8
    size = tiles.shape[0] // parts

    def kernel(tile_ref, *refs):
        out, done, sem = refs[len(after) :]
        copies = [
            pltpu.make_async_copy(tile_ref.at[pl.ds(k * size, size)], out.at[pl.ds(k * size, size)], sem.at[k])
            for k in range(parts)
        ]
        for copy in copies:
            copy.start()
        done[...] = jnp.zeros_like(done)
        for copy in copies:
            copy.wait()

    return pl.pallas_call(
        kernel,
        in_specs=[pl.BlockSpec(memory_space=pltpu.HBM)] + [pl.BlockSpec(memory_space=pl.ANY)] * len(after),
        out_specs=[pl.BlockSpec(memory_space=pltpu.VMEM)] * 2,
        out_shape=[pltpu.VMEM(tiles.shape, tiles.dtype), jax.ShapeDtypeStruct((8, 128), jnp.int32)],
        scratch_shapes=[pltpu.SemaphoreType.DMA((parts,))],
        compiler_params=pltpu.CompilerParams(vmem_limit_bytes=1 << 20),
        cost_estimate=pl.CostEstimate(flops=0, bytes_accessed=25 << 20, transcendentals=0),
        name="load_tiles",
    )(pltpu.with_memory_space_constraint(tiles, pltpu.HBM), *after)


def assemble(pieces):
    total = BLK + sum(piece.shape[0] for piece in pieces)

    def kernel(*refs):
        fill_slab(refs[-1], [(ref, 0, ref.shape[0]) for ref in refs[:-1]])

    vmem = pl.BlockSpec(memory_space=pltpu.VMEM)
    return pl.pallas_call(
        kernel,
        in_specs=[vmem] * len(pieces),
        out_specs=vmem,
        out_shape=pltpu.VMEM((total, pieces[0].shape[1]), BF),
        compiler_params=pltpu.CompilerParams(vmem_limit_bytes=8 << 20),
        name="assemble",
    )(*pieces)


def cut(one, three, *after):
    half = one.shape[0] // 2

    def kernel(one_ref, three_ref, *refs):
        first, second = refs[-2:]
        first[...] = one_ref[pl.ds(0, half)]
        second[...] = three_ref[pl.ds(half, half)]

    vmem = pl.BlockSpec(memory_space=pltpu.VMEM)
    return pl.pallas_call(
        kernel,
        in_specs=[vmem, vmem] + [pl.BlockSpec(memory_space=pl.ANY)] * len(after),
        out_specs=[vmem] * 2,
        out_shape=[shape(half)] * 2,
        compiler_params=pltpu.CompilerParams(vmem_limit_bytes=8 << 20),
        name="cut",
    )(one, three, *after)


def relay(values, after):
    n = len(values)

    def kernel(*refs):
        for k in range(n):
            refs[n + 1 + k][...] = refs[k][...]

    vmem = pl.BlockSpec(memory_space=pltpu.VMEM)
    return pl.pallas_call(
        kernel,
        in_specs=[vmem] * n + [pl.BlockSpec(memory_space=pl.ANY)],
        out_specs=[vmem] * n,
        out_shape=[shape(value.shape[0]) for value in values],
        compiler_params=pltpu.CompilerParams(vmem_limit_bytes=8 << 20),
        name="relay",
    )(*values, after)


def fill_slab(slab, pieces):
    slab[pl.ds(0, BLK)] = jnp.zeros((BLK, slab.shape[1]), BF)
    place = BLK
    for ref, row, rows in pieces:
        slab[pl.ds(place, rows)] = ref[pl.ds(row, rows)]
        place += rows


def aggregate(name, step, lists, pieces, tiles, outs, flipped, start=None, after=()):
    whole = len(pieces) == 1
    n_pieces = len(pieces)
    total = pieces[0][2] if whole else BLK + sum(rows for _, _, rows in pieces)
    blocks = max(first + size for first, size, _ in outs)
    direct = len(outs) == 1 and outs[0][2] == F32

    def kernel(listed, *refs):
        source = refs[:n_pieces]
        held = refs[n_pieces]
        refs = refs[n_pieces + 1 :]
        if start is not None:
            start_ref, refs = refs[0], refs[1:]
        refs = refs[len(after) :]
        out_refs, refs = refs[: len(outs)], refs[len(outs) :]
        acc = out_refs[0] if direct else refs[0]
        if whole:
            slab = source[0]
        else:
            slab = refs[-1]
            fill_slab(slab, [(ref, row, rows) for ref, (_, row, rows) in zip(source, pieces)])

        @pl.loop(0, blocks)
        def _(block):
            rows = pl.ds(pl.multiple_of(block * BLK, BLK), BLK)
            if start is None:
                acc[rows] = jnp.zeros((BLK, acc.shape[1]), F32)
            else:
                acc[rows] = start_ref[pl.ds(pl.multiple_of((block + start[1]) * BLK, BLK), BLK)]

        @pl.loop(listed[3, step], listed[3, step + 1])
        def _(group):
            for unit in range(UNROLL):
                spots = [group * GROUP + unit * UNIT + k for k in range(UNIT)]
                matrix = [held[listed[0, spot]] for spot in spots]
                read = [slab[pl.ds(pl.multiple_of(listed[1, spot] * BLK, BLK), BLK)] for spot in spots]
                to = pl.ds(pl.multiple_of(listed[2, spots[0]] * BLK, BLK), BLK)
                if flipped:
                    dims = (((0,), (0,)), ((), ()))
                    value = lax.dot_general(
                        jnp.concatenate(matrix, 0), jnp.concatenate(read, 0), dims, preferred_element_type=F32
                    )
                else:
                    value = jnp.dot(jnp.concatenate(matrix, 1), jnp.concatenate(read, 0), preferred_element_type=F32)
                acc[to] += value

        for out, (block, size, _) in zip(() if direct else out_refs, outs):

            @pl.loop(0, size)
            def _(k, out=out, block=block):
                rows = pl.ds(pl.multiple_of((block + k) * BLK, BLK), BLK)
                out[pl.ds(pl.multiple_of(k * BLK, BLK), BLK)] = acc[rows].astype(out.dtype)

    smem = pl.BlockSpec(memory_space=pltpu.SMEM)
    vmem = pl.BlockSpec(memory_space=pltpu.VMEM)
    width = pieces[0][0].shape[1]
    extra = [] if start is None else [start[0]]
    scratch = [] if direct else [pltpu.VMEM((blocks * BLK, width), F32)]
    if not whole:
        scratch.append(pltpu.VMEM((total, width), BF))
    return pl.pallas_call(
        kernel,
        in_specs=[smem] + [vmem] * (n_pieces + 1 + len(extra)) + [pl.BlockSpec(memory_space=pl.ANY)] * len(after),
        out_specs=[vmem] * len(outs),
        out_shape=[jax.ShapeDtypeStruct((size * BLK, width), dtype) for _, size, dtype in outs],
        scratch_shapes=scratch,
        compiler_params=pltpu.CompilerParams(vmem_limit_bytes=24 << 20),
        cost_estimate=pl.CostEstimate(flops=10**6, bytes_accessed=1 << 17, transcendentals=0),
        name=name,
    )(lists, *[array for array, _, _ in pieces], pltpu.with_memory_space_constraint(tiles, pltpu.VMEM), *extra, *after)


def local(name, body, out_shape, *operands):
    vmem = pl.BlockSpec(memory_space=pltpu.VMEM)
    return pl.pallas_call(
        body,
        in_specs=[vmem] * len(operands),
        out_specs=[vmem] * len(out_shape),
        out_shape=out_shape,
        compiler_params=pltpu.CompilerParams(vmem_limit_bytes=24 << 20),
        name=name,
    )(*operands)


def shape(rows, dtype=BF, width=256):
    return jax.ShapeDtypeStruct((rows, width), dtype)


def second_phase(half):
    def kernel(two, one, three, kept, *outs):
        total = kept[pl.ds(1024 * half, 1024)] + two[...].astype(F32) + (one[...].astype(F32) + three[...].astype(F32))
        for away, out in enumerate(outs):
            out[...] = total[256 * away : 256 * away + 256].astype(out.dtype)

    return kernel


SCALE = math.sqrt(2.0 / math.pi)


def dense(*refs):
    sums, (cotangent, weight, activated, message_a, message_b) = refs[:8], refs[8:]
    matrix = weight[...]
    halves = []
    for k in range(2):
        two, one, three, kept = sums[k::2]
        halves.append((kept[...] + two[...].astype(F32)) + (one[...].astype(F32) + three[...].astype(F32)))
    aggregated = jnp.concatenate(halves, 0).astype(BF)
    pre = jnp.dot(aggregated, matrix, preferred_element_type=F32)
    square = pre * pre
    curve = jnp.tanh(SCALE * (pre + 0.044715 * (pre * square)))
    activated[...] = (0.5 * pre * (1.0 + curve)).astype(BF)
    slope = 0.5 * (1.0 + curve) + 0.5 * pre * (1.0 - curve * curve) * (SCALE * (1.0 + 3.0 * 0.044715 * square))
    grad_pre = (cotangent[...].astype(F32) * slope).astype(BF)
    mixed = lax.dot_general(grad_pre, matrix, (((1,), (1,)), ((), ())), preferred_element_type=F32).astype(BF)
    grad = lax.dot_general(aggregated, grad_pre, (((0,), (0,)), ((), ())), preferred_element_type=F32).astype(BF)
    for k, message in enumerate((message_a, message_b)):
        for half in range(2):
            message[pl.ds(half * 192, BLK)] = mixed[(2 * k + half) * BLK : (2 * k + half + 1) * BLK]
            message[pl.ds(half * 192 + BLK, 64)] = grad[(2 * k + half) * 64 : (2 * k + half + 1) * 64]


def four(zero, one, two, three):
    return (zero.astype(F32) + two.astype(F32)) + (one.astype(F32) + three.astype(F32))


def gathered(two, three, one, own, out):
    for half in range(2):
        for slot, ref in enumerate((own, one, three, two)):
            out[pl.ds(half * 576 + slot * BLK, BLK)] = ref[pl.ds(192 * half, BLK)]
        parts = [ref[pl.ds(192 * half + BLK, 64)] for ref in (own, one, two, three)]
        out[pl.ds(half * 576 + 512, 64)] = four(*parts).astype(BF)


def sum_ring(*refs):
    out = refs[-1]
    for k in range(2):
        own, one, three, *two = refs[5 * k : 5 * k + 5]
        for half in range(2):
            rows = pl.ds(576 * half + 512, 64)
            total = four(own[rows], one[rows], two[half][pl.ds(512, 64)], three[rows])
            out[pl.ds((2 * k + half) * 64, 64)] = total


def last_phase(own, received, grad, grad_received, kept, one, two, three):
    total = own[...] + received[...].astype(F32)
    both = (grad[...] + grad_received[...]).astype(BF)
    kept[...] = total[0:512]
    for away, out in ((1, one), (2, two), (3, three)):
        out[pl.ds(0, 512)] = total[512 * away : 512 * away + 512].astype(BF)
        out[pl.ds(512, 256)] = both


def last_sum(two, one, three, kept, own, features, weight):
    rows, grads = pl.ds(0, 512), pl.ds(512, 256)
    total = (kept[...] + two[rows].astype(F32)) + (one[rows].astype(F32) + three[rows].astype(F32))
    features[...] = total.astype(BF)
    weight[...] = four(own[grads], one[grads], two[grads], three[grads])


def per_device(features, weight, cotangent, tile_values, tile_rows, tile_cols, tile_count):
    tiles = tile_values[0, 0]
    near_one, near_two = swap(features, "x", ONE), swap(features, "x", TWO)
    across = swap_core(features)
    row, col = lax.axis_index("row"), lax.axis_index("col")
    position = jnp.stack([row // 2, row % 2, col // 4, col % 4]).astype(jnp.int32)
    forward, backward = plan(position, tile_count, tile_rows[0], tile_cols[0])

    far_away = swap(features, "x", FAR)
    held_tiles, loaded = load(tiles, forward, backward)
    (far_away,) = relay((far_away,), loaded)
    across_near = [swap_core(near_one), swap_core(near_two)]
    held = [features, near_one, near_two, far_away, across, *across_near, swap_core(far_away)]
    slab = assemble(held)
    pieces = [(slab, 0, slab.shape[0])]

    def ways(axis, one, three, two):
        return swap(one, axis, ONE), swap(three, axis, TWO), swap(two, axis, FAR)

    def out(*dtypes):
        return [(8 * k, 8, dtype) for k, dtype in enumerate(dtypes)]

    def forward_part(step, name, outs, *after):
        return aggregate(name, step, forward, pieces, held_tiles, outs, False, None, after)

    a_two, b_two = far = forward_part(0, "forward_far", out(BF, BF))
    a_two, b_two = swap(a_two, "z", FAR), swap(b_two, "y", FAR)
    b_one, b_three = near_b = forward_part(1, "forward_near_b", out(BF, BF), far[0])
    b_one, b_three = swap(b_one, "y", ONE), swap(b_three, "y", TWO)
    a_one, a_three = near_a = forward_part(2, "forward_near_a", out(BF, BF), near_b[0])
    a_one, a_three = swap(a_one, "z", ONE), swap(a_three, "z", TWO)
    (kept,) = forward_part(3, "forward_own", [(0, 16, F32)], near_a[0], a_two, b_two)
    shapes = [shape(256, F32), shape(256), shape(256), shape(256)]
    a_own, a_one, a_two, a_three = local("second_phase_a", second_phase(0), shapes, a_two, a_one, a_three, kept)
    b_own, b_one, b_two, b_three = local("second_phase_b", second_phase(1), shapes, b_two, b_one, b_three, kept)
    a_one, a_three, a_two = ways("y", a_one, a_three, a_two)
    b_one, b_three, b_two = ways("z", b_one, b_three, b_two)
    activated, a_own, b_own = local(
        "dense", dense, [shape(512), shape(384), shape(384)], a_two, b_two, a_one, b_one, a_three, b_three, a_own, b_own, cotangent, weight
    )

    def spread(axis, own):
        two = swap(own, axis, FAR)
        three = swap(own, axis, TWO)
        return [two, three, swap(own, axis, ONE), own]

    a_held, b_held = spread("y", a_own), spread("z", b_own)
    (a_own,) = local("gathered_a", gathered, [shape(1152)], *a_held)
    a_one, a_three = swap(a_own, "z", ONE), swap(a_own, "z", TWO)
    (b_own,) = local("gathered_b", gathered, [shape(1152)], *b_held)
    b_one, b_three = swap(b_own, "y", ONE), swap(b_own, "y", TWO)
    here = [(piece, row, 512) for piece in (a_own, b_own) for row in (0, 576)]
    (sums,) = aggregate("backward_here", 0, backward, here, held_tiles, [(0, 32, F32)], True)
    a_first, a_second = cut(a_one, a_three, sums)
    b_first, b_second = cut(b_one, b_three, sums)
    a_far = swap(a_first, "z", TWO), swap(a_second, "z", ONE)
    b_far = swap(b_first, "y", TWO), swap(b_second, "y", ONE)

    near = [
        (piece, row, 512) for piece in (a_one, a_three, b_one, b_three) for row in (0, 576)
    ]
    distant = [(piece, 0, 512) for piece in (*a_far, *b_far)]
    (sums,) = aggregate("backward_near", 1, backward, near, held_tiles, [(0, 32, F32)], True, (sums, 0))
    (other_sum,) = aggregate("backward_other", 2, backward, distant, held_tiles, [(0, 16, BF)], True, (sums, 0))
    received = swap_core(other_sum)
    (grad,) = local(
        "sum_ring", sum_ring, [shape(256, F32)], a_own, a_one, a_three, *a_far, b_own, b_one, b_three, *b_far
    )
    grad_received = swap_core(grad)
    (own_sum,) = aggregate("backward_own", 3, backward, distant, held_tiles, [(0, 16, F32)], True, (sums, 16))
    kept, by_one, by_two, by_three = local(
        "last_phase", last_phase, [shape(512, F32), shape(768), shape(768), shape(768)],
        own_sum, received, grad, grad_received,
    )
    one, three, two = ways("x", by_one, by_three, by_two)
    grad_features, grad_weight = local(
        "last_sum", last_sum, [shape(512), shape(256, F32)], two, one, three, kept, by_one
    )
    return activated, grad_features, grad_weight


def solution(mesh):
    in_specs = (
        P(("row", "col"), None),
        P(),
        P(("row", "col"), None),
        P("row", "col", None, None, None),
        P("row", "col", None),
        P("row", "col", None),
        P("row", "col"),
    )
    out_specs = (P(("row", "col"), None), P(("row", "col"), None), P())
    return jax.shard_map(
        per_device, mesh=mesh, in_specs=in_specs, out_specs=out_specs, check_vma=False
    )
```

```python
import math

import jax
import jax.numpy as jnp
from jax import lax
from jax.experimental import pallas as pl
from jax.experimental.pallas import tpu as pltpu
from jax.sharding import PartitionSpec as P

BF = jnp.bfloat16
F32 = jnp.float32
BLK = 128
UNIT = 2
UNROLL = 8
GROUP = UNIT * UNROLL

ONE = ((0, 1), (1, 0), (2, 3), (3, 2))
TWO = ((1, 2), (2, 1), (3, 0), (0, 3))
FAR = ((0, 2), (2, 0), (1, 3), (3, 1))


def swap(value, axis, pairs):
    if axis == "z":
        return lax.ppermute(value, "col", [(y * 4 + a, y * 4 + b) for y in range(4) for a, b in pairs])
    if axis == "y":
        return lax.ppermute(value, "col", [(a * 4 + z, b * 4 + z) for z in range(4) for a, b in pairs])
    return lax.ppermute(value, "row", [(a * 2 + k, b * 2 + k) for k in range(2) for a, b in pairs])


def swap_core(value):
    return lax.ppermute(value, "row", [(2 * x + k, 2 * x + 1 - k) for x in range(4) for k in range(2)])


def distance(here, there):
    return ((1 - 2 * (here & 1)) * (there - here)) & 3


def pick(index, table):
    found = jnp.zeros_like(index)
    for place, entry in enumerate(table):
        found = jnp.where(index == place, entry, found)
    return found


ROLE = (6, 1, 0, 4, 7, 5, 2, 3)


FORWARD = ((0, 16), (16, 32), (32, 48), (48, 64))
BACKWARD = ((0, 32), (32, 64), (64, 80), (80, 96))
ROOM = 640


def sort_tiles(out, keys, source, live, segments):
    total, n_keys = keys.shape[1], segments[-1][1]

    def iota(rows, lanes, axis):
        return lax.broadcasted_iota(jnp.int32, (rows, lanes), axis).astype(F32)

    def column(value):
        return jnp.transpose(jnp.broadcast_to(value, (128, total)))

    def segment_of(key):
        return sum((key >= first).astype(F32) for first, _ in segments) - 1.0

    local = keys
    for first, _ in segments[1:]:
        local = jnp.where(keys >= first, keys - first, local)
    slots = lax.broadcasted_iota(jnp.int32, (1, total), 1)
    payload = (slots + 512 * (source + 1) + 65536 * (local + 1)).astype(F32)
    keys = jnp.where(live, keys, n_keys).astype(F32)
    key_column = column(keys)
    lane = iota(1, 128, 1)
    count = jnp.sum(jnp.where(key_column == lane, 1.0, 0.0), 0, keepdims=True)
    padded = jnp.where(lane < n_keys, ((count.astype(jnp.int32) + 1) >> 1 << 1).astype(F32), 0.0)
    bounds = [jnp.zeros((1, 1), F32)]
    for index in range(len(segments)):
        size = jnp.sum(jnp.where(segment_of(lane) == index, padded, 0.0), 1, keepdims=True).astype(jnp.int32)
        bounds.append(bounds[-1] + ((size + GROUP - 1) // GROUP).astype(F32))
    key, before = iota(n_keys, 128, 0), iota(n_keys, 128, 1)
    counted = (before < key) & (segment_of(before) == segment_of(key))
    offset = jnp.sum(jnp.where(counted, padded, 0.0), 1, keepdims=True)
    for index in range(len(segments)):
        offset += jnp.where(segment_of(key[:, :1]) == index, GROUP * bounds[index], 0.0)
    same = jnp.concatenate([key_column] * (total // 128), 1) == keys
    rank = jnp.sum(jnp.where(same & (iota(total, total, 0) < iota(total, total, 1)), 1.0, 0.0), 0, keepdims=True)
    start = jnp.sum(jnp.where(iota(n_keys, total, 0) == keys, offset, 0.0), 0, keepdims=True)
    place_column = column(jnp.where(live, rank + start, -1.0))
    payload_column = column(payload)
    for block in range(ROOM // 128):
        here = pl.ds(block * 128, 128)
        found = jnp.sum(jnp.where(place_column == lane + 128.0 * block, payload_column, 0.0), 0, keepdims=True)
        found = found.astype(jnp.int32)
        out[0:1, here] = found & 511
        out[1:2, here] = (found >> 9) & 127
        out[2:3, here] = jnp.where(found == 0, 0, (found >> 16) - 1)
        out[3:4, here] = sum(jnp.where(lane >= index, bounds[index] - bounds[index - 1], 0.0) for index in range(1, len(bounds))).astype(jnp.int32)


def plan(position, count, rows, cols):
    def kernel(position_ref, count_ref, rows_ref, cols_ref, forward, backward):
        x, core, y, z = [position_ref[k] for k in range(4)]
        rows, cols = rows_ref[...], cols_ref[...]
        live = lax.broadcasted_iota(jnp.int32, rows.shape, 1) < count_ref[0, 0]
        y_away, z_away = distance(y, rows >> 4), distance(z, (rows >> 2) & 3)
        second = (rows & 2) != 0
        half = rows & 1
        ring_one, ring_two = jnp.where(second, y_away, z_away), jnp.where(second, z_away, y_away)
        base = jnp.where(second, pick(ring_one, (56, 16, 8, 24)), pick(ring_one, (48, 32, 0, 40)))
        x_away, other = distance(x, cols >> 3), ((cols >> 2) & 1) ^ core
        slot = x_away ^ (x_away >> 1)
        source = other * 16 + slot * 4 + (cols & 3)
        sort_tiles(forward, base + ring_two * 2 + half, source, live, FORWARD)
        far = ring_one == 2
        near = ring_one % 2 == 1
        inner = ring_two ^ (ring_two >> 1)
        source = jnp.where(near, jnp.where(second, 16, 0) + (ring_one >> 1) * 8, jnp.where(second, 8, 0))
        source += half * 4 + inner
        role = pick(((cols >> 1) & 1) * 4 + x_away, ROLE)
        keys = jnp.where(far, 64, jnp.where(near, 32, 0)) + (1 - other) * 16 + role * 2 + (cols & 1)
        sort_tiles(backward, keys, source, live, BACKWARD)

    smem = pl.BlockSpec(memory_space=pltpu.SMEM)
    vmem = pl.BlockSpec(memory_space=pltpu.VMEM)
    return pl.pallas_call(
        kernel,
        in_specs=[smem, smem, vmem, vmem],
        out_specs=[vmem] * 2,
        out_shape=[jax.ShapeDtypeStruct((4, ROOM), jnp.int32)] * 2,
        compiler_params=pltpu.CompilerParams(vmem_limit_bytes=8 << 20),
        name="plan",
    )(position, count, rows, cols)


def load(tiles, *after):
    parts = 8
    size = tiles.shape[0] // parts

    def kernel(tile_ref, *refs):
        out, done, sem = refs[len(after) :]
        copies = [
            pltpu.make_async_copy(tile_ref.at[pl.ds(k * size, size)], out.at[pl.ds(k * size, size)], sem.at[k])
            for k in range(parts)
        ]
        for copy in copies:
            copy.start()
        done[...] = jnp.zeros_like(done)
        for copy in copies:
            copy.wait()

    return pl.pallas_call(
        kernel,
        in_specs=[pl.BlockSpec(memory_space=pltpu.HBM)] + [pl.BlockSpec(memory_space=pl.ANY)] * len(after),
        out_specs=[pl.BlockSpec(memory_space=pltpu.VMEM)] * 2,
        out_shape=[pltpu.VMEM(tiles.shape, tiles.dtype), jax.ShapeDtypeStruct((8, 128), jnp.int32)],
        scratch_shapes=[pltpu.SemaphoreType.DMA((parts,))],
        compiler_params=pltpu.CompilerParams(vmem_limit_bytes=1 << 20),
        cost_estimate=pl.CostEstimate(flops=0, bytes_accessed=25 << 20, transcendentals=0),
        name="load_tiles",
    )(pltpu.with_memory_space_constraint(tiles, pltpu.HBM), *after)


def assemble(pieces):
    total = BLK + sum(piece.shape[0] for piece in pieces)

    def kernel(*refs):
        fill_slab(refs[-1], [(ref, 0, ref.shape[0]) for ref in refs[:-1]])

    vmem = pl.BlockSpec(memory_space=pltpu.VMEM)
    return pl.pallas_call(
        kernel,
        in_specs=[vmem] * len(pieces),
        out_specs=vmem,
        out_shape=pltpu.VMEM((total, pieces[0].shape[1]), BF),
        compiler_params=pltpu.CompilerParams(vmem_limit_bytes=8 << 20),
        name="assemble",
    )(*pieces)


def cut(one, three, *after):
    half = one.shape[0] // 2

    def kernel(one_ref, three_ref, *refs):
        first, second = refs[-2:]
        first[...] = one_ref[pl.ds(0, half)]
        second[...] = three_ref[pl.ds(half, half)]

    vmem = pl.BlockSpec(memory_space=pltpu.VMEM)
    return pl.pallas_call(
        kernel,
        in_specs=[vmem, vmem] + [pl.BlockSpec(memory_space=pl.ANY)] * len(after),
        out_specs=[vmem] * 2,
        out_shape=[shape(half)] * 2,
        compiler_params=pltpu.CompilerParams(vmem_limit_bytes=8 << 20),
        name="cut",
    )(one, three, *after)


def relay(values, after):
    n = len(values)

    def kernel(*refs):
        for k in range(n):
            refs[n + 1 + k][...] = refs[k][...]

    vmem = pl.BlockSpec(memory_space=pltpu.VMEM)
    return pl.pallas_call(
        kernel,
        in_specs=[vmem] * n + [pl.BlockSpec(memory_space=pl.ANY)],
        out_specs=[vmem] * n,
        out_shape=[shape(value.shape[0]) for value in values],
        compiler_params=pltpu.CompilerParams(vmem_limit_bytes=8 << 20),
        name="relay",
    )(*values, after)


def fill_slab(slab, pieces):
    slab[pl.ds(0, BLK)] = jnp.zeros((BLK, slab.shape[1]), BF)
    place = BLK
    for ref, row, rows in pieces:
        slab[pl.ds(place, rows)] = ref[pl.ds(row, rows)]
        place += rows


def aggregate(name, step, lists, pieces, tiles, outs, flipped, start=None, after=()):
    whole = len(pieces) == 1
    n_pieces = len(pieces)
    total = pieces[0][2] if whole else BLK + sum(rows for _, _, rows in pieces)
    blocks = max(first + size for first, size, _ in outs)
    direct = len(outs) == 1 and outs[0][2] == F32

    def kernel(listed, *refs):
        source = refs[:n_pieces]
        held = refs[n_pieces]
        refs = refs[n_pieces + 1 :]
        if start is not None:
            start_ref, refs = refs[0], refs[1:]
        refs = refs[len(after) :]
        out_refs, refs = refs[: len(outs)], refs[len(outs) :]
        acc = out_refs[0] if direct else refs[0]
        if whole:
            slab = source[0]
        else:
            slab = refs[-1]
            fill_slab(slab, [(ref, row, rows) for ref, (_, row, rows) in zip(source, pieces)])

        @pl.loop(0, blocks)
        def _(block):
            rows = pl.ds(pl.multiple_of(block * BLK, BLK), BLK)
            if start is None:
                acc[rows] = jnp.zeros((BLK, acc.shape[1]), F32)
            else:
                acc[rows] = start_ref[pl.ds(pl.multiple_of((block + start[1]) * BLK, BLK), BLK)]

        @pl.loop(listed[3, step], listed[3, step + 1])
        def _(group):
            for unit in range(UNROLL):
                spots = [group * GROUP + unit * UNIT + k for k in range(UNIT)]
                matrix = [held[listed[0, spot]] for spot in spots]
                read = [slab[pl.ds(pl.multiple_of(listed[1, spot] * BLK, BLK), BLK)] for spot in spots]
                to = pl.ds(pl.multiple_of(listed[2, spots[0]] * BLK, BLK), BLK)
                if flipped:
                    dims = (((0,), (0,)), ((), ()))
                    value = lax.dot_general(
                        jnp.concatenate(matrix, 0), jnp.concatenate(read, 0), dims, preferred_element_type=F32
                    )
                else:
                    value = jnp.dot(jnp.concatenate(matrix, 1), jnp.concatenate(read, 0), preferred_element_type=F32)
                acc[to] += value

        for out, (block, size, _) in zip(() if direct else out_refs, outs):

            @pl.loop(0, size)
            def _(k, out=out, block=block):
                rows = pl.ds(pl.multiple_of((block + k) * BLK, BLK), BLK)
                out[pl.ds(pl.multiple_of(k * BLK, BLK), BLK)] = acc[rows].astype(out.dtype)

    smem = pl.BlockSpec(memory_space=pltpu.SMEM)
    vmem = pl.BlockSpec(memory_space=pltpu.VMEM)
    width = pieces[0][0].shape[1]
    extra = [] if start is None else [start[0]]
    scratch = [] if direct else [pltpu.VMEM((blocks * BLK, width), F32)]
    if not whole:
        scratch.append(pltpu.VMEM((total, width), BF))
    return pl.pallas_call(
        kernel,
        in_specs=[smem] + [vmem] * (n_pieces + 1 + len(extra)) + [pl.BlockSpec(memory_space=pl.ANY)] * len(after),
        out_specs=[vmem] * len(outs),
        out_shape=[jax.ShapeDtypeStruct((size * BLK, width), dtype) for _, size, dtype in outs],
        scratch_shapes=scratch,
        compiler_params=pltpu.CompilerParams(vmem_limit_bytes=24 << 20),
        cost_estimate=pl.CostEstimate(flops=10**6, bytes_accessed=1 << 17, transcendentals=0),
        name=name,
    )(lists, *[array for array, _, _ in pieces], pltpu.with_memory_space_constraint(tiles, pltpu.VMEM), *extra, *after)


def local(name, body, out_shape, *operands):
    vmem = pl.BlockSpec(memory_space=pltpu.VMEM)
    return pl.pallas_call(
        body,
        in_specs=[vmem] * len(operands),
        out_specs=[vmem] * len(out_shape),
        out_shape=out_shape,
        compiler_params=pltpu.CompilerParams(vmem_limit_bytes=24 << 20),
        name=name,
    )(*operands)


def shape(rows, dtype=BF, width=256):
    return jax.ShapeDtypeStruct((rows, width), dtype)


def second_phase(half):
    def kernel(two, one, three, kept, *outs):
        total = kept[pl.ds(1024 * half, 1024)] + two[...].astype(F32) + (one[...].astype(F32) + three[...].astype(F32))
        for away, out in enumerate(outs):
            out[...] = total[256 * away : 256 * away + 256].astype(out.dtype)

    return kernel


SCALE = math.sqrt(2.0 / math.pi)


def dense(*refs):
    sums, (cotangent, weight, activated, message_a, message_b) = refs[:8], refs[8:]
    matrix = weight[...]
    halves = []
    for k in range(2):
        two, one, three, kept = sums[k::2]
        halves.append((kept[...] + two[...].astype(F32)) + (one[...].astype(F32) + three[...].astype(F32)))
    aggregated = jnp.concatenate(halves, 0).astype(BF)
    pre = jnp.dot(aggregated, matrix, preferred_element_type=F32)
    square = pre * pre
    curve = jnp.tanh(SCALE * (pre + 0.044715 * (pre * square)))
    activated[...] = (0.5 * pre * (1.0 + curve)).astype(BF)
    slope = 0.5 * (1.0 + curve) + 0.5 * pre * (1.0 - curve * curve) * (SCALE * (1.0 + 3.0 * 0.044715 * square))
    grad_pre = (cotangent[...].astype(F32) * slope).astype(BF)
    mixed = lax.dot_general(grad_pre, matrix, (((1,), (1,)), ((), ())), preferred_element_type=F32).astype(BF)
    grad = lax.dot_general(aggregated, grad_pre, (((0,), (0,)), ((), ())), preferred_element_type=F32).astype(BF)
    for k, message in enumerate((message_a, message_b)):
        for half in range(2):
            message[pl.ds(half * 192, BLK)] = mixed[(2 * k + half) * BLK : (2 * k + half + 1) * BLK]
            message[pl.ds(half * 192 + BLK, 64)] = grad[(2 * k + half) * 64 : (2 * k + half + 1) * 64]


def four(zero, one, two, three):
    return (zero.astype(F32) + two.astype(F32)) + (one.astype(F32) + three.astype(F32))


def gathered(two, three, one, own, out):
    for half in range(2):
        for slot, ref in enumerate((own, one, three, two)):
            out[pl.ds(half * 576 + slot * BLK, BLK)] = ref[pl.ds(192 * half, BLK)]
        parts = [ref[pl.ds(192 * half + BLK, 64)] for ref in (own, one, two, three)]
        out[pl.ds(half * 576 + 512, 64)] = four(*parts).astype(BF)


def sum_ring(*refs):
    out = refs[-1]
    for k in range(2):
        own, one, three, *two = refs[5 * k : 5 * k + 5]
        for half in range(2):
            rows = pl.ds(576 * half + 512, 64)
            total = four(own[rows], one[rows], two[half][pl.ds(512, 64)], three[rows])
            out[pl.ds((2 * k + half) * 64, 64)] = total


def last_phase(own, received, grad, grad_received, by_one, by_two, late_two, late_one, kept):
    total = own[...] + received[...].astype(F32)
    by_one[pl.ds(0, 512)] = total[0:512].astype(BF)
    by_two[pl.ds(0, 512)] = total[512:1024].astype(BF)
    late_two[...] = total[1024:1280].astype(BF)
    late_one[...] = total[1280:1536].astype(BF)
    kept[...] = total[1536:2048]
    both = (grad[...] + grad_received[...]).astype(BF)
    by_one[pl.ds(512, 128)] = both[:128]
    by_two[pl.ds(512, 128)] = both[128:]


def last_forward(late_two, by_one, own_one, late_one, by_two, own_two, out_two, out_one):
    grads = pl.ds(512, 128)
    for late, got, own, out in ((late_two, by_one, own_one, out_two), (late_one, by_two, own_two, out_one)):
        out[pl.ds(0, 256)] = (late[...].astype(F32) + got[pl.ds(0, 256)].astype(F32)).astype(BF)
        out[pl.ds(256, 128)] = (own[grads].astype(F32) + got[grads].astype(F32)).astype(BF)


def last_sum(kept, by_one, by_two, late_two, late_one, own_late_two, own_late_one, features, weight):
    first = kept[pl.ds(0, 256)] + (by_one[pl.ds(256, 256)].astype(F32) + late_two[pl.ds(0, 256)].astype(F32))
    second = kept[pl.ds(256, 256)] + (by_two[pl.ds(256, 256)].astype(F32) + late_one[pl.ds(0, 256)].astype(F32))
    features[pl.ds(0, 256)] = first.astype(BF)
    features[pl.ds(256, 256)] = second.astype(BF)
    rows = pl.ds(256, 128)
    weight[pl.ds(0, 128)] = own_late_two[rows].astype(F32) + late_two[rows].astype(F32)
    weight[pl.ds(128, 128)] = own_late_one[rows].astype(F32) + late_one[rows].astype(F32)


def per_device(features, weight, cotangent, tile_values, tile_rows, tile_cols, tile_count):
    tiles = tile_values[0, 0]
    near_one, near_two = swap(features, "x", ONE), swap(features, "x", TWO)
    across = swap_core(features)
    row, col = lax.axis_index("row"), lax.axis_index("col")
    position = jnp.stack([row // 2, row % 2, col // 4, col % 4]).astype(jnp.int32)
    forward, backward = plan(position, tile_count, tile_rows[0], tile_cols[0])

    far_away = swap(features, "x", FAR)
    held_tiles, loaded = load(tiles, forward, backward)
    (far_away,) = relay((far_away,), loaded)
    across_near = [swap_core(near_one), swap_core(near_two)]
    held = [features, near_one, near_two, far_away, across, *across_near, swap_core(far_away)]
    slab = assemble(held)
    pieces = [(slab, 0, slab.shape[0])]

    def ways(axis, one, three, two):
        return swap(one, axis, ONE), swap(three, axis, TWO), swap(two, axis, FAR)

    def out(*dtypes):
        return [(8 * k, 8, dtype) for k, dtype in enumerate(dtypes)]

    def forward_part(step, name, outs, *after):
        return aggregate(name, step, forward, pieces, held_tiles, outs, False, None, after)

    a_two, b_two = far = forward_part(0, "forward_far", out(BF, BF))
    a_two, b_two = swap(a_two, "z", FAR), swap(b_two, "y", FAR)
    b_one, b_three = near_b = forward_part(1, "forward_near_b", out(BF, BF), far[0])
    b_one, b_three = swap(b_one, "y", ONE), swap(b_three, "y", TWO)
    a_one, a_three = near_a = forward_part(2, "forward_near_a", out(BF, BF), near_b[0])
    a_one, a_three = swap(a_one, "z", ONE), swap(a_three, "z", TWO)
    (kept,) = forward_part(3, "forward_own", [(0, 16, F32)], near_a[0], a_two, b_two)
    shapes = [shape(256, F32), shape(256), shape(256), shape(256)]
    a_own, a_one, a_two, a_three = local("second_phase_a", second_phase(0), shapes, a_two, a_one, a_three, kept)
    b_own, b_one, b_two, b_three = local("second_phase_b", second_phase(1), shapes, b_two, b_one, b_three, kept)
    a_one, a_three, a_two = ways("y", a_one, a_three, a_two)
    b_one, b_three, b_two = ways("z", b_one, b_three, b_two)
    activated, a_own, b_own = local(
        "dense", dense, [shape(512), shape(384), shape(384)], a_two, b_two, a_one, b_one, a_three, b_three, a_own, b_own, cotangent, weight
    )

    def spread(axis, own):
        two = swap(own, axis, FAR)
        three = swap(own, axis, TWO)
        return [two, three, swap(own, axis, ONE), own]

    a_held, b_held = spread("y", a_own), spread("z", b_own)
    (a_own,) = local("gathered_a", gathered, [shape(1152)], *a_held)
    a_one, a_three = swap(a_own, "z", ONE), swap(a_own, "z", TWO)
    (b_own,) = local("gathered_b", gathered, [shape(1152)], *b_held)
    b_one, b_three = swap(b_own, "y", ONE), swap(b_own, "y", TWO)
    here = [(piece, row, 512) for piece in (a_own, b_own) for row in (0, 576)]
    (sums,) = aggregate("backward_here", 0, backward, here, held_tiles, [(0, 32, F32)], True)
    a_first, a_second = cut(a_one, a_three, sums)
    b_first, b_second = cut(b_one, b_three, sums)
    a_far = swap(a_first, "z", TWO), swap(a_second, "z", ONE)
    b_far = swap(b_first, "y", TWO), swap(b_second, "y", ONE)

    near = [
        (piece, row, 512) for piece in (a_one, a_three, b_one, b_three) for row in (0, 576)
    ]
    distant = [(piece, 0, 512) for piece in (*a_far, *b_far)]
    (sums,) = aggregate("backward_near", 1, backward, near, held_tiles, [(0, 32, F32)], True, (sums, 0))
    (other_sum,) = aggregate("backward_other", 2, backward, distant, held_tiles, [(0, 16, BF)], True, (sums, 0))
    received = swap_core(other_sum)
    (grad,) = local(
        "sum_ring", sum_ring, [shape(256, F32)], a_own, a_one, a_three, *a_far, b_own, b_one, b_three, *b_far
    )
    grad_received = swap_core(grad)
    (own_sum,) = aggregate("backward_own", 3, backward, distant, held_tiles, [(0, 16, F32)], True, (sums, 16))
    by_one, by_two, late_two, late_one, kept = local(
        "last_phase", last_phase, [shape(640), shape(640), shape(256), shape(256), shape(512, F32)],
        own_sum, received, grad, grad_received,
    )
    got_one, got_two = swap(by_one, "x", ONE), swap(by_two, "x", TWO)
    own_two, own_one = local(
        "last_forward", last_forward, [shape(384), shape(384)],
        late_two, got_one, by_one, late_one, got_two, by_two,
    )
    late_two, late_one = swap(own_two, "x", TWO), swap(own_one, "x", ONE)
    grad_features, grad_weight = local(
        "last_sum", last_sum, [shape(512), shape(256, F32)],
        kept, got_one, got_two, late_two, late_one, own_two, own_one,
    )
    return activated, grad_features, grad_weight


def solution(mesh):
    in_specs = (
        P(("row", "col"), None),
        P(),
        P(("row", "col"), None),
        P("row", "col", None, None, None),
        P("row", "col", None),
        P("row", "col", None),
        P("row", "col"),
    )
    out_specs = (P(("row", "col"), None), P(("row", "col"), None), P())
    return jax.shard_map(
        per_device, mesh=mesh, in_specs=in_specs, out_specs=out_specs, check_vma=False
    )
```

```python
import math

import jax
import jax.numpy as jnp
from jax import lax
from jax.experimental import pallas as pl
from jax.experimental.pallas import tpu as pltpu
from jax.sharding import PartitionSpec as P

BF = jnp.bfloat16
F32 = jnp.float32
BLK = 128
UNIT = 2
UNROLL = 8
GROUP = UNIT * UNROLL

ONE = ((0, 1), (1, 0), (2, 3), (3, 2))
TWO = ((1, 2), (2, 1), (3, 0), (0, 3))
FAR = ((0, 2), (2, 0), (1, 3), (3, 1))


def swap(value, axis, pairs):
    if axis == "z":
        return lax.ppermute(value, "col", [(y * 4 + a, y * 4 + b) for y in range(4) for a, b in pairs])
    if axis == "y":
        return lax.ppermute(value, "col", [(a * 4 + z, b * 4 + z) for z in range(4) for a, b in pairs])
    return lax.ppermute(value, "row", [(a * 2 + k, b * 2 + k) for k in range(2) for a, b in pairs])


def swap_core(value):
    return lax.ppermute(value, "row", [(2 * x + k, 2 * x + 1 - k) for x in range(4) for k in range(2)])


def distance(here, there):
    return ((1 - 2 * (here & 1)) * (there - here)) & 3


def pick(index, table):
    found = jnp.zeros_like(index)
    for place, entry in enumerate(table):
        found = jnp.where(index == place, entry, found)
    return found


ROLE = (6, 1, 0, 4, 7, 5, 2, 3)


FORWARD = ((0, 16), (16, 48), (48, 64))
BACKWARD = ((0, 32), (32, 64), (64, 80), (80, 96))
ROOM = 640


def sort_tiles(out, keys, source, live, segments):
    total, n_keys = keys.shape[1], segments[-1][1]

    def iota(rows, lanes, axis):
        return lax.broadcasted_iota(jnp.int32, (rows, lanes), axis).astype(F32)

    def column(value):
        return jnp.transpose(jnp.broadcast_to(value, (128, total)))

    def segment_of(key):
        return sum((key >= first).astype(F32) for first, _ in segments) - 1.0

    local = keys
    for first, _ in segments[1:]:
        local = jnp.where(keys >= first, keys - first, local)
    slots = lax.broadcasted_iota(jnp.int32, (1, total), 1)
    payload = (slots + 512 * (source + 1) + 65536 * (local + 1)).astype(F32)
    keys = jnp.where(live, keys, n_keys).astype(F32)
    key_column = column(keys)
    lane = iota(1, 128, 1)
    count = jnp.sum(jnp.where(key_column == lane, 1.0, 0.0), 0, keepdims=True)
    padded = jnp.where(lane < n_keys, ((count.astype(jnp.int32) + 1) >> 1 << 1).astype(F32), 0.0)
    bounds = [jnp.zeros((1, 1), F32)]
    for index in range(len(segments)):
        size = jnp.sum(jnp.where(segment_of(lane) == index, padded, 0.0), 1, keepdims=True).astype(jnp.int32)
        bounds.append(bounds[-1] + ((size + GROUP - 1) // GROUP).astype(F32))
    key, before = iota(n_keys, 128, 0), iota(n_keys, 128, 1)
    counted = (before < key) & (segment_of(before) == segment_of(key))
    offset = jnp.sum(jnp.where(counted, padded, 0.0), 1, keepdims=True)
    for index in range(len(segments)):
        offset += jnp.where(segment_of(key[:, :1]) == index, GROUP * bounds[index], 0.0)
    same = jnp.concatenate([key_column] * (total // 128), 1) == keys
    rank = jnp.sum(jnp.where(same & (iota(total, total, 0) < iota(total, total, 1)), 1.0, 0.0), 0, keepdims=True)
    start = jnp.sum(jnp.where(iota(n_keys, total, 0) == keys, offset, 0.0), 0, keepdims=True)
    place_column = column(jnp.where(live, rank + start, -1.0))
    payload_column = column(payload)
    for block in range(ROOM // 128):
        here = pl.ds(block * 128, 128)
        found = jnp.sum(jnp.where(place_column == lane + 128.0 * block, payload_column, 0.0), 0, keepdims=True)
        found = found.astype(jnp.int32)
        out[0:1, here] = found & 511
        out[1:2, here] = (found >> 9) & 127
        out[2:3, here] = jnp.where(found == 0, 0, (found >> 16) - 1)
        out[3:4, here] = sum(jnp.where(lane >= index, bounds[index] - bounds[index - 1], 0.0) for index in range(1, len(bounds))).astype(jnp.int32)


def plan(position, count, rows, cols):
    def kernel(position_ref, count_ref, rows_ref, cols_ref, forward, backward):
        x, core, y, z = [position_ref[k] for k in range(4)]
        rows, cols = rows_ref[...], cols_ref[...]
        live = lax.broadcasted_iota(jnp.int32, rows.shape, 1) < count_ref[0, 0]
        y_away, z_away = distance(y, rows >> 4), distance(z, (rows >> 2) & 3)
        second = (rows & 2) != 0
        half = rows & 1
        ring_one, ring_two = jnp.where(second, y_away, z_away), jnp.where(second, z_away, y_away)
        base = jnp.where(second, pick(ring_one, (56, 16, 8, 24)), pick(ring_one, (48, 32, 0, 40)))
        x_away, other = distance(x, cols >> 3), ((cols >> 2) & 1) ^ core
        slot = x_away ^ (x_away >> 1)
        source = other * 16 + slot * 4 + (cols & 3)
        sort_tiles(forward, base + ring_two * 2 + half, source, live, FORWARD)
        far = ring_one == 2
        near = ring_one % 2 == 1
        inner = ring_two ^ (ring_two >> 1)
        source = jnp.where(near, jnp.where(second, 16, 0) + (ring_one >> 1) * 8, jnp.where(second, 8, 0))
        source += half * 4 + inner
        role = pick(((cols >> 1) & 1) * 4 + x_away, ROLE)
        keys = jnp.where(far, 64, jnp.where(near, 32, 0)) + (1 - other) * 16 + role * 2 + (cols & 1)
        sort_tiles(backward, keys, source, live, BACKWARD)

    smem = pl.BlockSpec(memory_space=pltpu.SMEM)
    vmem = pl.BlockSpec(memory_space=pltpu.VMEM)
    return pl.pallas_call(
        kernel,
        in_specs=[smem, smem, vmem, vmem],
        out_specs=[vmem] * 2,
        out_shape=[jax.ShapeDtypeStruct((4, ROOM), jnp.int32)] * 2,
        compiler_params=pltpu.CompilerParams(vmem_limit_bytes=8 << 20),
        name="plan",
    )(position, count, rows, cols)


def load(tiles, *after):
    parts = 8
    size = tiles.shape[0] // parts

    def kernel(tile_ref, *refs):
        out, done, sem = refs[len(after) :]
        copies = [
            pltpu.make_async_copy(tile_ref.at[pl.ds(k * size, size)], out.at[pl.ds(k * size, size)], sem.at[k])
            for k in range(parts)
        ]
        for copy in copies:
            copy.start()
        done[...] = jnp.zeros_like(done)
        for copy in copies:
            copy.wait()

    return pl.pallas_call(
        kernel,
        in_specs=[pl.BlockSpec(memory_space=pltpu.HBM)] + [pl.BlockSpec(memory_space=pl.ANY)] * len(after),
        out_specs=[pl.BlockSpec(memory_space=pltpu.VMEM)] * 2,
        out_shape=[pltpu.VMEM(tiles.shape, tiles.dtype), jax.ShapeDtypeStruct((8, 128), jnp.int32)],
        scratch_shapes=[pltpu.SemaphoreType.DMA((parts,))],
        compiler_params=pltpu.CompilerParams(vmem_limit_bytes=1 << 20),
        cost_estimate=pl.CostEstimate(flops=0, bytes_accessed=25 << 20, transcendentals=0),
        name="load_tiles",
    )(pltpu.with_memory_space_constraint(tiles, pltpu.HBM), *after)


def assemble(pieces):
    total = BLK + sum(piece.shape[0] for piece in pieces)

    def kernel(*refs):
        fill_slab(refs[-1], [(ref, 0, ref.shape[0]) for ref in refs[:-1]])

    vmem = pl.BlockSpec(memory_space=pltpu.VMEM)
    return pl.pallas_call(
        kernel,
        in_specs=[vmem] * len(pieces),
        out_specs=vmem,
        out_shape=pltpu.VMEM((total, pieces[0].shape[1]), BF),
        compiler_params=pltpu.CompilerParams(vmem_limit_bytes=8 << 20),
        name="assemble",
    )(*pieces)


def cut(one, three, *after):
    half = one.shape[0] // 2

    def kernel(one_ref, three_ref, *refs):
        first, second = refs[-2:]
        first[...] = one_ref[pl.ds(0, half)]
        second[...] = three_ref[pl.ds(half, half)]

    vmem = pl.BlockSpec(memory_space=pltpu.VMEM)
    return pl.pallas_call(
        kernel,
        in_specs=[vmem, vmem] + [pl.BlockSpec(memory_space=pl.ANY)] * len(after),
        out_specs=[vmem] * 2,
        out_shape=[shape(half)] * 2,
        compiler_params=pltpu.CompilerParams(vmem_limit_bytes=8 << 20),
        name="cut",
    )(one, three, *after)


def relay(values, after):
    n = len(values)

    def kernel(*refs):
        for k in range(n):
            refs[n + 1 + k][...] = refs[k][...]

    vmem = pl.BlockSpec(memory_space=pltpu.VMEM)
    return pl.pallas_call(
        kernel,
        in_specs=[vmem] * n + [pl.BlockSpec(memory_space=pl.ANY)],
        out_specs=[vmem] * n,
        out_shape=[shape(value.shape[0]) for value in values],
        compiler_params=pltpu.CompilerParams(vmem_limit_bytes=8 << 20),
        name="relay",
    )(*values, after)


def fill_slab(slab, pieces):
    slab[pl.ds(0, BLK)] = jnp.zeros((BLK, slab.shape[1]), BF)
    place = BLK
    for ref, row, rows in pieces:
        slab[pl.ds(place, rows)] = ref[pl.ds(row, rows)]
        place += rows


def aggregate(name, step, lists, pieces, tiles, outs, flipped, start=None, after=()):
    whole = len(pieces) == 1
    n_pieces = len(pieces)
    total = pieces[0][2] if whole else BLK + sum(rows for _, _, rows in pieces)
    blocks = max(first + size for first, size, _ in outs)
    direct = len(outs) == 1 and outs[0][2] == F32

    def kernel(listed, *refs):
        source = refs[:n_pieces]
        held = refs[n_pieces]
        refs = refs[n_pieces + 1 :]
        if start is not None:
            start_ref, refs = refs[0], refs[1:]
        refs = refs[len(after) :]
        out_refs, refs = refs[: len(outs)], refs[len(outs) :]
        acc = out_refs[0] if direct else refs[0]
        if whole:
            slab = source[0]
        else:
            slab = refs[-1]
            fill_slab(slab, [(ref, row, rows) for ref, (_, row, rows) in zip(source, pieces)])

        @pl.loop(0, blocks)
        def _(block):
            rows = pl.ds(pl.multiple_of(block * BLK, BLK), BLK)
            if start is None:
                acc[rows] = jnp.zeros((BLK, acc.shape[1]), F32)
            else:
                acc[rows] = start_ref[pl.ds(pl.multiple_of((block + start[1]) * BLK, BLK), BLK)]

        @pl.loop(listed[3, step], listed[3, step + 1])
        def _(group):
            for unit in range(UNROLL):
                spots = [group * GROUP + unit * UNIT + k for k in range(UNIT)]
                matrix = [held[listed[0, spot]] for spot in spots]
                read = [slab[pl.ds(pl.multiple_of(listed[1, spot] * BLK, BLK), BLK)] for spot in spots]
                to = pl.ds(pl.multiple_of(listed[2, spots[0]] * BLK, BLK), BLK)
                if flipped:
                    dims = (((0,), (0,)), ((), ()))
                    value = lax.dot_general(
                        jnp.concatenate(matrix, 0), jnp.concatenate(read, 0), dims, preferred_element_type=F32
                    )
                else:
                    value = jnp.dot(jnp.concatenate(matrix, 1), jnp.concatenate(read, 0), preferred_element_type=F32)
                acc[to] += value

        for out, (block, size, _) in zip(() if direct else out_refs, outs):

            @pl.loop(0, size)
            def _(k, out=out, block=block):
                rows = pl.ds(pl.multiple_of((block + k) * BLK, BLK), BLK)
                out[pl.ds(pl.multiple_of(k * BLK, BLK), BLK)] = acc[rows].astype(out.dtype)

    smem = pl.BlockSpec(memory_space=pltpu.SMEM)
    vmem = pl.BlockSpec(memory_space=pltpu.VMEM)
    width = pieces[0][0].shape[1]
    extra = [] if start is None else [start[0]]
    scratch = [] if direct else [pltpu.VMEM((blocks * BLK, width), F32)]
    if not whole:
        scratch.append(pltpu.VMEM((total, width), BF))
    return pl.pallas_call(
        kernel,
        in_specs=[smem] + [vmem] * (n_pieces + 1 + len(extra)) + [pl.BlockSpec(memory_space=pl.ANY)] * len(after),
        out_specs=[vmem] * len(outs),
        out_shape=[jax.ShapeDtypeStruct((size * BLK, width), dtype) for _, size, dtype in outs],
        scratch_shapes=scratch,
        compiler_params=pltpu.CompilerParams(vmem_limit_bytes=24 << 20),
        cost_estimate=pl.CostEstimate(flops=10**6, bytes_accessed=1 << 17, transcendentals=0),
        name=name,
    )(lists, *[array for array, _, _ in pieces], pltpu.with_memory_space_constraint(tiles, pltpu.VMEM), *extra, *after)


def local(name, body, out_shape, *operands):
    vmem = pl.BlockSpec(memory_space=pltpu.VMEM)
    return pl.pallas_call(
        body,
        in_specs=[vmem] * len(operands),
        out_specs=[vmem] * len(out_shape),
        out_shape=out_shape,
        compiler_params=pltpu.CompilerParams(vmem_limit_bytes=24 << 20),
        name=name,
    )(*operands)


def shape(rows, dtype=BF, width=256):
    return jax.ShapeDtypeStruct((rows, width), dtype)


def second_phase(half):
    def kernel(two, one, three, kept, *outs):
        total = kept[pl.ds(1024 * half, 1024)] + two[...].astype(F32) + (one[...].astype(F32) + three[...].astype(F32))
        for away, out in enumerate(outs):
            out[...] = total[256 * away : 256 * away + 256].astype(out.dtype)

    return kernel


SCALE = math.sqrt(2.0 / math.pi)


def dense(*refs):
    sums, (cotangent, weight, activated, message_a, message_b) = refs[:8], refs[8:]
    matrix = weight[...]
    halves = []
    for k in range(2):
        two, one, three, kept = sums[k::2]
        halves.append((kept[...] + two[...].astype(F32)) + (one[...].astype(F32) + three[...].astype(F32)))
    aggregated = jnp.concatenate(halves, 0).astype(BF)
    pre = jnp.dot(aggregated, matrix, preferred_element_type=F32)
    square = pre * pre
    curve = jnp.tanh(SCALE * (pre + 0.044715 * (pre * square)))
    activated[...] = (0.5 * pre * (1.0 + curve)).astype(BF)
    slope = 0.5 * (1.0 + curve) + 0.5 * pre * (1.0 - curve * curve) * (SCALE * (1.0 + 3.0 * 0.044715 * square))
    grad_pre = (cotangent[...].astype(F32) * slope).astype(BF)
    mixed = lax.dot_general(grad_pre, matrix, (((1,), (1,)), ((), ())), preferred_element_type=F32).astype(BF)
    grad = lax.dot_general(aggregated, grad_pre, (((0,), (0,)), ((), ())), preferred_element_type=F32).astype(BF)
    for k, message in enumerate((message_a, message_b)):
        for half in range(2):
            message[pl.ds(half * 192, BLK)] = mixed[(2 * k + half) * BLK : (2 * k + half + 1) * BLK]
            message[pl.ds(half * 192 + BLK, 64)] = grad[(2 * k + half) * 64 : (2 * k + half + 1) * 64]


def four(zero, one, two, three):
    return (zero.astype(F32) + two.astype(F32)) + (one.astype(F32) + three.astype(F32))


def gathered(two, three, one, own, out):
    for half in range(2):
        for slot, ref in enumerate((own, one, three, two)):
            out[pl.ds(half * 576 + slot * BLK, BLK)] = ref[pl.ds(192 * half, BLK)]
        parts = [ref[pl.ds(192 * half + BLK, 64)] for ref in (own, one, two, three)]
        out[pl.ds(half * 576 + 512, 64)] = four(*parts).astype(BF)


def sum_ring(*refs):
    out = refs[-1]
    for k in range(2):
        own, one, three, *two = refs[5 * k : 5 * k + 5]
        for half in range(2):
            rows = pl.ds(576 * half + 512, 64)
            total = four(own[rows], one[rows], two[half][pl.ds(512, 64)], three[rows])
            out[pl.ds((2 * k + half) * 64, 64)] = total


def last_phase(own, received, grad, grad_received, by_one, by_two, late_two, late_one, kept):
    total = own[...] + received[...].astype(F32)
    by_one[pl.ds(0, 512)] = total[0:512].astype(BF)
    by_two[pl.ds(0, 512)] = total[512:1024].astype(BF)
    late_two[...] = total[1024:1280].astype(BF)
    late_one[...] = total[1280:1536].astype(BF)
    kept[...] = total[1536:2048]
    both = (grad[...] + grad_received[...]).astype(BF)
    by_one[pl.ds(512, 128)] = both[:128]
    by_two[pl.ds(512, 128)] = both[128:]


def last_forward(late_two, by_one, own_one, late_one, by_two, own_two, out_two, out_one):
    grads = pl.ds(512, 128)
    for late, got, own, out in ((late_two, by_one, own_one, out_two), (late_one, by_two, own_two, out_one)):
        out[pl.ds(0, 256)] = (late[...].astype(F32) + got[pl.ds(0, 256)].astype(F32)).astype(BF)
        out[pl.ds(256, 128)] = (own[grads].astype(F32) + got[grads].astype(F32)).astype(BF)


def last_sum(kept, by_one, by_two, late_two, late_one, own_late_two, own_late_one, features, weight):
    first = kept[pl.ds(0, 256)] + (by_one[pl.ds(256, 256)].astype(F32) + late_two[pl.ds(0, 256)].astype(F32))
    second = kept[pl.ds(256, 256)] + (by_two[pl.ds(256, 256)].astype(F32) + late_one[pl.ds(0, 256)].astype(F32))
    features[pl.ds(0, 256)] = first.astype(BF)
    features[pl.ds(256, 256)] = second.astype(BF)
    rows = pl.ds(256, 128)
    weight[pl.ds(0, 128)] = own_late_two[rows].astype(F32) + late_two[rows].astype(F32)
    weight[pl.ds(128, 128)] = own_late_one[rows].astype(F32) + late_one[rows].astype(F32)


def per_device(features, weight, cotangent, tile_values, tile_rows, tile_cols, tile_count):
    tiles = tile_values[0, 0]
    near_one, near_two = swap(features, "x", ONE), swap(features, "x", TWO)
    across = swap_core(features)
    row, col = lax.axis_index("row"), lax.axis_index("col")
    position = jnp.stack([row // 2, row % 2, col // 4, col % 4]).astype(jnp.int32)
    forward, backward = plan(position, tile_count, tile_rows[0], tile_cols[0])

    far_away = swap(features, "x", FAR)
    held_tiles, loaded = load(tiles, forward, backward)
    (far_away,) = relay((far_away,), loaded)
    across_near = [swap_core(near_one), swap_core(near_two)]
    held = [features, near_one, near_two, far_away, across, *across_near, swap_core(far_away)]
    slab = assemble(held)
    pieces = [(slab, 0, slab.shape[0])]

    def ways(axis, one, three, two):
        return swap(one, axis, ONE), swap(three, axis, TWO), swap(two, axis, FAR)

    def out(*dtypes):
        return [(8 * k, 8, dtype) for k, dtype in enumerate(dtypes)]

    def forward_part(step, name, outs, *after):
        return aggregate(name, step, forward, pieces, held_tiles, outs, False, None, after)

    a_two, b_two = far = forward_part(0, "forward_far", out(BF, BF))
    a_two, b_two = swap(a_two, "z", FAR), swap(b_two, "y", FAR)
    near = forward_part(1, "forward_near", out(BF, BF, BF, BF), far[0])
    b_one, b_three = swap(near[0], "y", ONE), swap(near[1], "y", TWO)
    a_one, a_three = swap(near[2], "z", ONE), swap(near[3], "z", TWO)
    (kept,) = forward_part(2, "forward_own", [(0, 16, F32)], near[0], a_two, b_two)
    shapes = [shape(256, F32), shape(256), shape(256), shape(256)]
    a_own, a_one, a_two, a_three = local("second_phase_a", second_phase(0), shapes, a_two, a_one, a_three, kept)
    b_own, b_one, b_two, b_three = local("second_phase_b", second_phase(1), shapes, b_two, b_one, b_three, kept)
    a_one, a_three, a_two = ways("y", a_one, a_three, a_two)
    b_one, b_three, b_two = ways("z", b_one, b_three, b_two)
    activated, a_own, b_own = local(
        "dense", dense, [shape(512), shape(384), shape(384)], a_two, b_two, a_one, b_one, a_three, b_three, a_own, b_own, cotangent, weight
    )

    def spread(axis, own):
        two = swap(own, axis, FAR)
        three = swap(own, axis, TWO)
        return [two, three, swap(own, axis, ONE), own]

    a_held, b_held = spread("y", a_own), spread("z", b_own)
    (a_own,) = local("gathered_a", gathered, [shape(1152)], *a_held)
    a_one, a_three = swap(a_own, "z", ONE), swap(a_own, "z", TWO)
    (b_own,) = local("gathered_b", gathered, [shape(1152)], *b_held)
    b_one, b_three = swap(b_own, "y", ONE), swap(b_own, "y", TWO)
    here = [(piece, row, 512) for piece in (a_own, b_own) for row in (0, 576)]
    (sums,) = aggregate("backward_here", 0, backward, here, held_tiles, [(0, 32, F32)], True)
    a_first, a_second = cut(a_one, a_three, sums)
    b_first, b_second = cut(b_one, b_three, sums)
    a_far = swap(a_first, "z", TWO), swap(a_second, "z", ONE)
    b_far = swap(b_first, "y", TWO), swap(b_second, "y", ONE)

    near = [
        (piece, row, 512) for piece in (a_one, a_three, b_one, b_three) for row in (0, 576)
    ]
    distant = [(piece, 0, 512) for piece in (*a_far, *b_far)]
    (sums,) = aggregate("backward_near", 1, backward, near, held_tiles, [(0, 32, F32)], True, (sums, 0))
    (other_sum,) = aggregate("backward_other", 2, backward, distant, held_tiles, [(0, 16, BF)], True, (sums, 0))
    received = swap_core(other_sum)
    (grad,) = local(
        "sum_ring", sum_ring, [shape(256, F32)], a_own, a_one, a_three, *a_far, b_own, b_one, b_three, *b_far
    )
    grad_received = swap_core(grad)
    (own_sum,) = aggregate("backward_own", 3, backward, distant, held_tiles, [(0, 16, F32)], True, (sums, 16))
    by_one, by_two, late_two, late_one, kept = local(
        "last_phase", last_phase, [shape(640), shape(640), shape(256), shape(256), shape(512, F32)],
        own_sum, received, grad, grad_received,
    )
    got_one, got_two = swap(by_one, "x", ONE), swap(by_two, "x", TWO)
    own_two, own_one = local(
        "last_forward", last_forward, [shape(384), shape(384)],
        late_two, got_one, by_one, late_one, got_two, by_two,
    )
    late_two, late_one = swap(own_two, "x", TWO), swap(own_one, "x", ONE)
    grad_features, grad_weight = local(
        "last_sum", last_sum, [shape(512), shape(256, F32)],
        kept, got_one, got_two, late_two, late_one, own_two, own_one,
    )
    return activated, grad_features, grad_weight


def solution(mesh):
    in_specs = (
        P(("row", "col"), None),
        P(),
        P(("row", "col"), None),
        P("row", "col", None, None, None),
        P("row", "col", None),
        P("row", "col", None),
        P("row", "col"),
    )
    out_specs = (P(("row", "col"), None), P(("row", "col"), None), P())
    return jax.shard_map(
        per_device, mesh=mesh, in_specs=in_specs, out_specs=out_specs, check_vma=False
    )
```
